32 devices in a mesh: dp: 8 (over z, y), tensor: 4 (over x, core).
Axes of the slice: x: 2, y: 2, z: 4, core: 2. Of those that a mesh axis runs over, the one named last changes fastest.
Arguments:
- hidden: float32 [16384, 1024], P(('dp', 'tensor')), may hold values from -6 to 6
- segment_ids: int32 [8, 2048], P('dp'), may hold values from 0 to 4, never falling along the last dimension, each value on 1 to 1024 neighbouring positions
- in_gain: bfloat16 [2, 1024], P(None, 'dp'), may hold values from 0.5 to 1.5
- w_zx: bfloat16 [2, 1024, 2, 2048], P(None, 'dp', None, 'tensor'), may hold values from -0.1875 to 0.1875
- w_bcdt: bfloat16 [2, 1024, 288], P(None, 'dp'), may hold values from -0.1875 to 0.1875
- w_out: bfloat16 [2, 1024, 2048], P(None, 'dp', 'tensor'), may hold values from -0.125 to 0.125
- conv_x: float32 [2, 4, 2048], P(None, None, 'tensor'), may hold values from -3 to 3
- conv_x_bias: float32 [2, 2048], P(None, 'tensor'), may hold values from -3 to 3
- conv_bc: float32 [2, 4, 256], replicated, may hold values from -3 to 3
- conv_bc_bias: float32 [2, 256], replicated, may hold values from -3 to 3
- dt_bias: float32 [2, 32], P(None, 'tensor'), may hold values from -6 to -2
- a_log: float32 [2, 32], P(None, 'tensor'), may hold values from -4 to 1
- d_skip: float32 [2, 32], P(None, 'tensor'), may hold values from 0.5 to 1.5
- out_gain: float32 [2, 2048], P(None, 'tensor'), may hold values from 0.5 to 1.5
- cotangent: float32 [16384, 1024], P(('dp', 'tensor')), may hold values from -6 to 6
Outputs:
- result: float32 [16384, 1024], P(('dp', 'tensor'))
- grad_hidden: float32 [16384, 1024], P(('dp', 'tensor'))
- grad_in_gain: float32 [2, 1024], P(None, ('dp', 'tensor'))
- grad_w_zx: float32 [2, 1024, 2, 2048], P(None, 'dp', None, 'tensor')
- grad_w_bcdt: float32 [2, 1024, 288], P(None, ('dp', 'tensor'))
- grad_w_out: float32 [2, 1024, 2048], P(None, 'dp', 'tensor')
- grad_conv_x: float32 [2, 4, 2048], P(None, None, 'tensor')
- grad_conv_x_bias: float32 [2, 2048], P(None, 'tensor')
- grad_conv_bc: float32 [2, 4, 256], replicated
- grad_conv_bc_bias: float32 [2, 256], replicated
- grad_dt_bias: float32 [2, 32], P(None, 'tensor')
- grad_a_log: float32 [2, 32], P(None, 'tensor')
- grad_d_skip: float32 [2, 32], P(None, 'tensor')
- grad_out_gain: float32 [2, 2048], P(None, 'tensor')
The draws below stay inside these ranges and needn't reach their ends.
All inputs are finite; a program needn't handle non-finite values.
Results may differ from the reference program's by a relative error of at most 0.03.
Values may be sent and summed in bfloat16 or wider, within the bound.
No kernel may reach another device: no remote copies, remote signals or barrier semaphores. Data moves between devices by JAX's collectives and lax.ppermute only.
A program may use at most 256 MiB of HBM per device.

```python
import math
import jax
import jax.numpy as jnp
import numpy as np
from jax import lax

D = 1024
INNER = 2048
STATE = 128
CONV = 4
SPAN = 256
LAYERS = 2
LEN = 2048
HEADS = 32
SEQS = 8
TOKENS = 16384


def levels(stream_key, shape, split, smallest, high):
    loudness, own = 1.0, jax.random.fold_in(stream_key, 6)
    for axis_at, parts in split:
        heights = jnp.exp(jax.random.uniform(jax.random.fold_in(own, axis_at), (parts,), jnp.float32, smallest / len(split), high / len(split)))
        loudness = loudness * jnp.repeat(heights, shape[axis_at] // parts).reshape([-1 if axis == axis_at else 1 for axis in range(len(shape))])
    return loudness


def length_profile(amount, total, bound, lean):
    loads = [(1 << 20) // math.isqrt(rank ** lean) + 1 for rank in range(2, amount + 1)]
    rest, counts = total - bound - (amount - 1), [1] * (amount - 1)
    while rest > 0:
        movable = [i for i in range(amount - 1) if counts[i] < bound]
        whole, remaining = sum([loads[i] for i in movable]), rest
        for i in movable:
            addition = min(bound - counts[i], max(1, remaining * loads[i] // whole), rest)
            counts[i] = counts[i] + addition
            rest = rest - addition
    return np.array([bound] + counts)


def ragged(rng, number_of, total, bound, slope):
    if number_of == 2:
        one = jax.random.randint(rng, (), max(1, total - bound), min(bound, total - 1) + 1)
        return jnp.stack([one, total - one])
    lengths = jnp.asarray(length_profile(number_of, total, bound, slope), jnp.int32)
    pairs = (number_of - 1) // 2
    giver, sink = lengths[1:1 + 2 * pairs:2], lengths[2:2 + 2 * pairs:2]
    margin = jnp.minimum(giver - 1, bound - sink)
    passed = jax.random.randint(jax.random.fold_in(rng, 1), (pairs,), 0, 1 << 20) % (margin + 1)
    lengths = lengths.at[1:1 + 2 * pairs:2].set(giver - passed).at[2:2 + 2 * pairs:2].set(sink + passed)
    return lengths[jax.random.permutation(jax.random.fold_in(rng, 2), number_of)]


def normal_values(own_key, dims, scale, reach, shards=(), dtype=jnp.bfloat16):
    gain = levels(own_key, dims, shards, -0.22, 0.18) if shards else 1.0
    entries = jax.random.normal(own_key, dims, jnp.float32) * scale * gain
    return jnp.minimum(jnp.maximum(entries, -reach), reach).astype(dtype)


def setup_inputs(seed: int = 0) -> dict:
    key_list = jax.random.split(jax.random.key(seed), 16)
    return {
        "hidden": normal_values(key_list[0], (TOKENS, D), 1.0, 6.0, ((0, 32),), jnp.float32),
        "segment_ids": jax.vmap(lambda own: jnp.searchsorted(jnp.cumsum(ragged(own, 5, LEN, LEN // 2, 0)), jnp.arange(LEN), side="right"))(jax.random.split(key_list[1], SEQS)).reshape((SEQS, LEN)).astype(jnp.int32),
        "in_gain": jnp.clip(1.0 + 0.1 * jax.random.normal(key_list[2], (LAYERS, D), jnp.float32), 0.5, 1.5).astype(jnp.bfloat16),
        "w_zx": normal_values(key_list[3], (LAYERS, D, 2, INNER), D ** -0.5, 0.1875, ((1, 8), (3, 4))),
        "w_bcdt": normal_values(key_list[4], (LAYERS, D, 2 * STATE + HEADS), D ** -0.5, 0.1875, ((1, 8),)),
        "w_out": normal_values(key_list[5], (LAYERS, D, INNER), INNER ** -0.5, 0.125, ((1, 8), (2, 4))),
        "conv_x": normal_values(key_list[6], (LAYERS, CONV, INNER), CONV ** -0.5, 3.0, ((2, 4),), jnp.float32),
        "conv_x_bias": normal_values(key_list[7], (LAYERS, INNER), 0.5, 3.0, ((1, 4),), jnp.float32),
        "conv_bc": normal_values(key_list[8], (LAYERS, CONV, 2 * STATE), CONV ** -0.5, 3.0, (), jnp.float32),
        "conv_bc_bias": normal_values(key_list[9], (LAYERS, 2 * STATE), 0.5, 3.0, (), jnp.float32),
        "dt_bias": jnp.clip(-6.0 + 4.0 * jax.random.uniform(key_list[10], (LAYERS, HEADS), jnp.float32) ** levels(key_list[10], (LAYERS, HEADS), ((1, 4),), -0.2, 0.2), -6.0, -2.0),
        "a_log": jnp.clip(-4.0 + 5.0 * jax.random.uniform(key_list[11], (LAYERS, HEADS), jnp.float32) ** levels(key_list[11], (LAYERS, HEADS), ((1, 4),), -0.2, 0.2), -4.0, 1.0),
        "d_skip": jnp.clip(0.5 + 1.0 * jax.random.uniform(key_list[12], (LAYERS, HEADS), jnp.float32) ** levels(key_list[12], (LAYERS, HEADS), ((1, 4),), -0.2, 0.2), 0.5, 1.5),
        "out_gain": jnp.clip(1.0 + 0.1 * jax.random.normal(key_list[13], (LAYERS, INNER), jnp.float32), 0.5, 1.5),
        "cotangent": normal_values(key_list[14], (TOKENS, D), 1.0, 6.0, ((0, 32),), jnp.float32),
    }


epsilon = 1e-05
highest = lax.Precision.HIGHEST

@jax.custom_vjp
def low(v):
    return lax.optimization_barrier(v.astype(jnp.bfloat16)).astype(jnp.float32)

@jax.custom_vjp
def low_back(v):
    return v

def low_keep(v):
    return (low(v), None)

def low_pass(kept, grad):
    return (grad,)

def back_keep(v):
    return (v, None)

def back_low(kept, grad):
    return (low(grad),)
low.defvjp(low_keep, low_pass)
low_back.defvjp(back_keep, back_low)

def conv_silu(values, weights, biases, segment):
    seq_len = values.shape[1]
    summed = biases + weights[0] * values
    for offset in range(1, weights.shape[0]):
        shifted = jnp.pad(values, ((0, 0), (offset, 0), (0, 0)))[:, :seq_len]
        earlier = jnp.pad(segment, ((0, 0), (offset, 0)), constant_values=-1)[:, :seq_len]
        keeping = (earlier == segment).astype(jnp.float32)[:, :, None]
        summed = summed + weights[offset] * shifted * keeping
    return jax.nn.silu(summed)

def ssd_scan(values, steps_dt, decay_rate, keys_b, reads_c, segment):
    seq_count, seq_len, head_count, head_dim = values.shape
    blocks = seq_len // SPAN

    def to_blocks(source):
        reshaped = source.reshape((seq_count, blocks, SPAN) + source.shape[2:])
        return jnp.moveaxis(reshaped, 1, 0)
    lower_tri = lax.broadcasted_iota(jnp.int32, (SPAN, SPAN), 0) >= lax.broadcasted_iota(jnp.int32, (SPAN, SPAN), 1)

    def block_step(carried_in, block_in):
        state_now, previous = carried_in
        block_x, block_dt, block_b, block_c, block_seg = block_in
        cumulative = jnp.cumsum(block_dt * decay_rate, axis=1)
        same_doc = (block_seg[:, :, None] == block_seg[:, None, :]) & lower_tri
        between = cumulative[:, :, None, :] - cumulative[:, None, :, :]
        mixing = jnp.where(same_doc[:, :, :, None], jnp.exp(jnp.minimum(between, 0.0)), 0.0)
        intersection = jnp.einsum('sin,sjn->sij', block_c, block_b, precision=highest)
        weighted = mixing * intersection[:, :, :, None] * block_dt[:, None, :, :]
        output = jnp.einsum('sijh,sjhp->sihp', weighted, block_x, precision=highest)
        carried = (block_seg == previous[:, None]).astype(jnp.float32)
        factor = jnp.exp(cumulative) * carried[:, :, None]
        output = output + jnp.einsum('sin,shpn->sihp', block_c, state_now, precision=highest) * factor[:, :, :, None]
        ending = jnp.exp(cumulative[:, -1:, :] - cumulative) * (block_seg == block_seg[:, -1:]).astype(jnp.float32)[:, :, None] * block_dt
        state_now = state_now * factor[:, -1][:, :, None, None] + jnp.einsum('sjh,sjhp,sjn->shpn', ending, block_x, block_b, precision=highest)
        return ((state_now, block_seg[:, -1]), output)
    initial = (jnp.zeros((seq_count, head_count, head_dim, keys_b.shape[-1]), jnp.float32), jnp.full((seq_count,), -1, jnp.int32))
    unused, outputs = lax.scan(jax.checkpoint(block_step), initial, (to_blocks(values), to_blocks(steps_dt), to_blocks(keys_b), to_blocks(reads_c), to_blocks(segment)))
    return jnp.moveaxis(outputs, 0, 1).reshape(values.shape)

def mixer(gate_z, inner_x, state_bc, step_pre, conv_xw, conv_xb, conv_bcw, conv_bcb, dt_shift, log_rate, skip_scale, segment):
    seq_count, seq_len = segment.shape
    row_count = gate_z.shape[0]
    head_count = step_pre.shape[1]
    conv_out = conv_silu(inner_x.reshape(seq_count, seq_len, -1), conv_xw, conv_xb, segment)
    state_in = conv_silu(state_bc.reshape(seq_count, seq_len, -1), conv_bcw, conv_bcb, segment)
    half_bc = state_in.shape[-1] // 2
    step_dt = jax.nn.softplus(step_pre.reshape(seq_count, seq_len, head_count) + dt_shift)
    heads_x = conv_out.reshape(seq_count, seq_len, head_count, -1)
    scanned = ssd_scan(heads_x, step_dt, -jnp.exp(log_rate), state_in[..., :half_bc], state_in[..., half_bc:], segment)
    scanned = scanned + skip_scale[:, None] * heads_x
    return scanned.reshape(row_count, -1) * jax.nn.silu(gate_z)

def layer(stream, in_scale, proj_zx, proj_bcdt, proj_out, conv_xw, conv_xb, conv_bcw, conv_bcb, dt_shift, log_rate, skip_scale, out_scale, segment):
    bc_width = conv_bcw.shape[1]
    inv_rms = lax.rsqrt(lax.optimization_barrier(jnp.mean(stream * stream, axis=-1, keepdims=True)) + epsilon)
    normed = low(stream * inv_rms * in_scale)
    both = low_back(jnp.einsum('td,dki->tki', normed, proj_zx, precision=highest))
    shared = low_back(jnp.dot(normed, proj_bcdt, precision=highest))
    gated = mixer(both[:, 0], both[:, 1], shared[:, :bc_width], shared[:, bc_width:], conv_xw, conv_xb, conv_bcw, conv_bcb, dt_shift, log_rate, skip_scale, segment)
    gate_rms = lax.rsqrt(lax.optimization_barrier(jnp.mean(gated * gated, axis=-1, keepdims=True)) + epsilon)
    mixed = low(gated * gate_rms * out_scale)
    branch = low_back(jnp.einsum('ti,di->td', mixed, proj_out, precision=highest))
    return stream + branch

def reference(hidden, segment_ids, in_gain, w_zx, w_bcdt, w_out, conv_x, conv_x_bias, conv_bc, conv_bc_bias, dt_bias, a_log, d_skip, out_gain, cotangent):
    params = tuple((p.astype(jnp.float32) for p in (in_gain, w_zx, w_bcdt, w_out, conv_x, conv_x_bias, conv_bc, conv_bc_bias, dt_bias, a_log, d_skip, out_gain)))
    group_size = 2 if SEQS % 2 == 0 else 1
    groups = SEQS // group_size
    streams = hidden.astype(jnp.float32).reshape(groups, group_size * LEN, D)
    cotangents = cotangent.astype(jnp.float32).reshape(groups, group_size * LEN, D)
    segments = segment_ids.reshape(groups, group_size, LEN)

    def one_group(accumulated, group_in):
        stream, cot_rows, segment = group_in

        def forward(start_rows, weights_all):
            current = start_rows
            for layer_at in range(LAYERS):
                current = layer(current, *[p[layer_at] for p in weights_all], segment)
            return current
        output, pullback = jax.vjp(forward, stream, params)
        grad_rows, grad_params = pullback(cot_rows)
        accumulated = jax.tree.map(lambda left, right: left + right, accumulated, grad_params)
        return (accumulated, (output, grad_rows))
    zeroes = jax.tree.map(jnp.zeros_like, params)
    grads, (outputs, grad_rows) = lax.scan(one_group, zeroes, (streams, cotangents, segments))
    return (outputs.reshape(TOKENS, D), grad_rows.reshape(TOKENS, D), grads[0], grads[1], grads[2], grads[3], grads[4], grads[5], grads[6], grads[7], grads[8], grads[9], grads[10], grads[11])
```

```python
from functools import partial

import jax
import jax.numpy as jnp
from jax import lax
from jax.experimental import pallas as pl
from jax.experimental.pallas import tpu as pltpu
from jax.sharding import PartitionSpec as P

bf16 = jnp.bfloat16
f32 = jnp.float32
epsilon = 1e-05
SPAN = 256
HALO = 16
LANES = 128
NEG = -1e30
VMEM = 56 * 1024 * 1024


def mm(a, b):
    return lax.dot_general(a, b, (((1,), (0,)), ((), ())), preferred_element_type=f32)


def mmt(a, b):
    return lax.dot_general(a, b, (((1,), (1,)), ((), ())), preferred_element_type=f32)


def mmf(a, b):
    return lax.dot_general(
        a, b, (((1,), (0,)), ((), ())), precision=lax.Precision.HIGHEST, preferred_element_type=f32
    )


def two(x):
    first = low(x)
    return first, low(x - first.astype(f32))


def mm3(a, b):
    a0, a1 = two(a)
    b0, b1 = two(b)
    return mm(a0, b0) + (mm(a0, b1) + mm(a1, b0))


def mmt3(a, b):
    a0, a1 = two(a)
    b0, b1 = two(b)
    return mmt(a0, b0) + (mmt(a0, b1) + mmt(a1, b0))


def iota(shape, axis):
    return lax.broadcasted_iota(jnp.int32, shape, axis)


def low(x):
    return x.astype(bf16)


def three(x):
    first = low(x).astype(f32)
    rest = x - first
    second = low(rest).astype(f32)
    return first, second, rest - second


def split_heads(x, heads):
    first, second, third = three(x)
    part = iota(x.shape, 1) // heads
    zero = jnp.zeros_like(x)
    return low(
        jnp.where(part == 0, first, jnp.where(part == 1, second, jnp.where(part == 2, third, zero)))
    )


def spread(group, heads, own, width):
    row, col = iota((LANES, width), 0), iota((LANES, width), 1)
    return low(
        ((row % heads == group * own + col // (width // own)) & (row < 3 * heads)).astype(f32)
    )


def pick(group, heads, own):
    row, col = iota((LANES, LANES), 0), iota((LANES, LANES), 1)
    return low(((row % heads == group * own + col) & (col < own) & (row < 3 * heads)).astype(f32))


def gather_heads(x, group, own):
    width = x.shape[1]
    row, col = iota((width, LANES), 0), iota((width, LANES), 1)
    fold = low((col == group * own + row // (width // own)).astype(f32))
    first, second, third = three(x)
    return mm(low(first), fold) + mm(low(second), fold) + mm(low(third), fold)


def keeps(segc, rows):
    now = segc[HALO : HALO + rows]
    return [None] + [
        (segc[HALO - j : HALO - j + rows] == now).astype(f32) for j in range(1, 4)
    ]


def conv(ext, taps, keep, rows, count):
    total = taps[count : count + 1] + taps[0:1] * ext[HALO : HALO + rows]
    for j in range(1, count):
        total = total + taps[j : j + 1] * (ext[HALO - j : HALO - j + rows] * keep[j])
    return total


def triangle(rows, lower):
    row, col = iota((rows, rows), 0), iota((rows, rows), 1)
    return ((row >= col) if lower else (row <= col)).astype(f32)


def scan_in_kernel(
    heads,
    own,
    taps_n,
    nrm,
    w,
    wb,
    prm,
    cbc,
    hp,
    segc,
    segr,
    y,
    xin,
    state,
    ftot,
    shared,
    b_out,
    c_out,
    bt_out,
    ct_out,
    dtp_out,
    cumt_out,
    dts_out,
    es_out,
    fs_out,
    fd_out,
    cums_out,
    g_scr,
    m_scr,
):
    group = pl.program_id(0)
    rows = y.shape[0]
    width = y.shape[1]
    chunks = rows // SPAN
    keep = keeps(segc[...], rows)

    @pl.when(group == 0)
    def _():
        sh = mm(nrm[...], wb[...])
        shared[...] = sh
        half = cbc.shape[1] // 2
        act = conv(sh[:, : 2 * half], cbc[...], keep, rows, taps_n)
        act = act * jax.nn.sigmoid(act)
        bmat, cmat = act[:, :half], act[:, half:]
        b_out[...] = bmat
        c_out[...] = cmat
        bt_out[...] = bmat.T
        ct_out[...] = cmat.T
        dtp = sh[HALO:, 2 * half :] + hp[0:1]
        dtp_out[...] = dtp
        dt = jnp.maximum(dtp, 0.0) + jnp.log1p(jnp.exp(-jnp.abs(dtp)))
        cum = mmf(triangle(rows, True), dt * hp[1:2])
        cumt_out[...] = cum.T
        dts_out[...] = split_heads(dt, heads)
        cums_out[...] = split_heads(cum, heads)
        seg = segc[...]
        here = seg[HALO:]
        fd_out[...] = split_heads(
            jnp.exp(cum) * (here == seg[HALO - 1 : HALO]).astype(f32), heads
        )
        for c in range(chunks):
            lo, hi = c * SPAN, (c + 1) * SPAN
            block = cum[lo:hi]
            base = jnp.zeros_like(cum[0:1]) if c == 0 else cum[lo - 1 : lo]
            before = seg[HALO + lo - 1 : HALO + lo]
            last = here[hi - 1 : hi]
            fs_out[lo:hi] = split_heads(
                jnp.exp(block - base) * (here[lo:hi] == before).astype(f32), heads
            )
            es_out[lo:hi] = split_heads(
                jnp.exp(cum[hi - 1 : hi] - block) * (here[lo:hi] == last).astype(f32), heads
            )
            g_scr[c] = mmt3(cmat[lo:hi], bmat[lo:hi])
            ok = (here[lo:hi] == segr[0:1, lo:hi]) & (
                iota((SPAN, SPAN), 0) >= iota((SPAN, SPAN), 1)
            )
            m_scr[c] = jnp.where(ok, 0.0, NEG)

    weight = w[...].reshape(-1, width)
    ext = mm(nrm[...], weight)
    xin[...] = ext
    u = conv(ext, prm[0], keep, rows, taps_n)
    xc = u * jax.nn.sigmoid(u)
    grow = spread(group, heads, own, width)
    xd = xc * mm(dts_out[...], grow)
    xd0, xd1 = two(xd)
    exd = xd * mm(es_out[...], grow)
    fx = mm(fs_out[...], grow)
    cols = mm(cums_out[...], pick(group, heads, own))
    rowsum = cumt_out[pl.ds(pl.multiple_of(group * own, own), own), :]
    per = width // own
    side = iota((SPAN, 2 * per), 1) < per
    now = None
    for c in range(chunks):
        lo, hi = c * SPAN, (c + 1) * SPAN
        m, g = m_scr[c], g_scr[c]
        for pair in range(own // 2):
            at = slice(2 * per * pair, 2 * per * (pair + 1))
            x2 = jnp.concatenate([xd0[lo:hi, at], xd1[lo:hi, at]], axis=1)
            out = []
            for h in (2 * pair, 2 * pair + 1):
                decay = jnp.exp(cols[lo:hi, h : h + 1] - rowsum[h : h + 1, lo:hi] + m)
                both = mm(low(decay * g), x2)
                out.append(both[:, : 2 * per] + both[:, 2 * per :])
            y[lo:hi, at] = (
                jnp.where(side, out[0], out[1]) + prm[0, 6:7, at] * xc[lo:hi, at]
            )
        local = mm3(bt_out[:, lo:hi], exd[lo:hi])
        if c > 0:
            y[lo:hi] += fx[lo:hi] * mm3(c_out[lo:hi], now)
            now = fx[hi - 1 : hi] * now + local
        else:
            now = local
    state[...] = low(now)
    ftot[...] = jnp.broadcast_to(mm(fd_out[...], grow)[rows - 1 : rows], ftot.shape)


def gate_kernel(
    heads,
    own,
    full,
    nrm,
    wz,
    wo,
    y_loc,
    c_in,
    fd,
    s_in,
    prm,
    hid,
    z_out,
    y_out,
    branch,
    grms,
    nxt,
    ss,
):
    group = pl.program_id(0)
    width = y_loc.shape[1]
    z = mm(nrm[HALO:], wz[...].reshape(-1, width))
    y = y_loc[...] + mm(fd[...], spread(group, heads, own, width)) * (
        lambda parts: mm(parts[0], s_in[...]) + mm(parts[1], s_in[...])
    )(two(c_in[...]))
    z_out[...] = z
    y_out[...] = y
    gated = y * (z * jax.nn.sigmoid(z))
    squares = jnp.sum(gated * gated, axis=1, keepdims=True)
    part = mmt(low(gated * prm[0, 5:6]), wo[...].reshape(-1, width))

    @pl.when(group == 0)
    def _():
        ss[...] = jnp.broadcast_to(squares, ss.shape)
        branch[...] = part

    @pl.when(group > 0)
    def _():
        ss[...] += jnp.broadcast_to(squares, ss.shape)
        branch[...] += part

    @pl.when(group == pl.num_programs(0) - 1)
    def _():
        scale = lax.rsqrt(ss[...] / full + epsilon)
        grms[...] = scale
        total = branch[...] * scale[:, 0:1]
        branch[...] = total
        nxt[...] = hid[...] + total


def gate_back_kernel(
    heads,
    own,
    full,
    dbr,
    dbrt,
    branch,
    wo,
    wz,
    z_in,
    y_in,
    grms,
    nrmt,
    ct,
    fd,
    prm,
    g_out,
    g_z,
    dy_out,
    dn,
    dstate,
    g_gain,
    q_scr,
):
    group = pl.program_id(0)
    rows, width = z_in.shape

    @pl.when(group == 0)
    def _():
        inner = jnp.sum(dbr[...].astype(f32) * branch[...], axis=1, keepdims=True)
        q_scr[...] = grms[...] * grms[...] * (inner / full)

    rms = grms[:, 0:1]
    dm = mm(dbr[...], wo[...].reshape(-1, width))
    z, y = z_in[...], y_in[...]
    sg = jax.nn.sigmoid(z)
    sz = z * sg
    gated = y * sz
    scaled = gated * rms
    gain = prm[0, 5:6]
    g_out[...] = low(mm(dbrt[...], low(scaled * gain))).reshape(g_out.shape)
    g_gain[...] = jnp.broadcast_to(jnp.sum(dm * scaled, axis=0, keepdims=True), g_gain.shape)
    dg = rms * (dm * gain) - gated * q_scr[:, 0:1]
    dy = dg * sz
    dy_out[...] = dy
    dz = low(dg * y * (sg + sz * (1.0 - sg)))
    g_z[...] = low(mm(nrmt[:, :rows], dz)).reshape(g_z.shape)
    part = mmt(dz, wz[...].reshape(-1, width))

    @pl.when(group == 0)
    def _():
        dn[...] = part

    @pl.when(group > 0)
    def _():
        dn[...] += part

    dstate[...] = low(mm3(ct[...], mm(fd[...], spread(group, heads, own, width)) * dy))


def conv_back(du, ext, taps, keep, rows, count, dest):
    dest[...] = jnp.zeros_like(dest)
    dest[0:rows] = taps[0:1] * du
    sums = [jnp.sum(du * ext[HALO : HALO + rows], axis=0, keepdims=True)]
    for j in range(1, count):
        kept = du * keep[j]
        sums.append(jnp.sum(kept * ext[HALO - j : HALO - j + rows], axis=0, keepdims=True))
        moved = taps[j : j + 1] * kept
        dest[0 : rows - j] += moved[j:]
        dest[rows + HALO - j : rows + HALO] += moved[:j]
    return sums, jnp.sum(du, axis=0, keepdims=True)


def scan_back_kernel(
    heads,
    own,
    taps_n,
    xin,
    dy_in,
    y_in,
    s_in,
    ds_in,
    w,
    wb,
    prm,
    cbc,
    hp,
    segc,
    segr,
    nrmt,
    shared,
    b_in,
    c_in,
    bt,
    ct,
    dtp,
    cumt,
    dts,
    es,
    fs,
    cums,
    g_x,
    g_b,
    dn,
    g_prm,
    g_cbc,
    g_hp,
    gt_scr,
    mt_scr,
    dgt_scr,
    db_scr,
    dc_scr,
    dcum_scr,
    ddt_scr,
    dx_scr,
    dbc_scr,
    dxc_scr,
):
    group = pl.program_id(0)
    rows, width = dy_in.shape
    chunks = rows // SPAN
    keep = keeps(segc[...], rows)

    @pl.when(group == 0)
    def _():
        here = segc[HALO:]
        for c in range(chunks):
            lo, hi = c * SPAN, (c + 1) * SPAN
            gt_scr[c] = mmt3(b_in[lo:hi], c_in[lo:hi])
            ok = (here[lo:hi] == segr[0:1, lo:hi]) & (
                iota((SPAN, SPAN), 0) <= iota((SPAN, SPAN), 1)
            )
            mt_scr[c] = jnp.where(ok, 0.0, NEG)
        for ref in (dgt_scr, db_scr, dc_scr, dcum_scr, ddt_scr):
            ref[...] = jnp.zeros_like(ref)

    u = conv(xin[...], prm[0], keep, rows, taps_n)
    sg = jax.nn.sigmoid(u)
    xc = u * sg
    grow = spread(group, heads, own, width)
    dtx = mm(dts[...], grow)
    ex = mm(es[...], grow)
    fx = mm(fs[...], grow)
    xd = xc * dtx
    xd0, xd1 = two(xd)
    exd = xd * ex
    cols = mm(cums[...], pick(group, heads, own))
    rowsum = cumt[pl.ds(pl.multiple_of(group * own, own), own), :]
    dy = dy_in[...]
    dyb = low(dy)
    fdy = fx * dy
    skip = prm[0, 6:7]
    per = width // own
    side = iota((SPAN, 2 * per), 1) < per
    wide_side = (iota((SPAN, 4 * per), 1) // per) % 2 == 0
    states = [s_in[...].astype(f32)]
    for c in range(chunks - 1):
        lo, hi = c * SPAN, (c + 1) * SPAN
        states.append(fx[hi - 1 : hi] * states[-1] + mm3(bt[:, lo:hi], exd[lo:hi]))
    ds = ds_in[...].astype(f32)
    for c in reversed(range(chunks)):
        lo, hi = c * SPAN, (c + 1) * SPAN
        dxs = ex[lo:hi] * mm3(b_in[lo:hi], ds)
        db_scr[lo:hi] += mmt3(exd[lo:hi], ds)
        dc_scr[lo:hi] += mmt3(fdy[lo:hi], states[c])
        mt, gt = mt_scr[c], gt_scr[c]
        parts = []
        dgt = None
        for pair in range(own // 2):
            at = slice(2 * per * pair, 2 * per * (pair + 1))
            x2 = jnp.concatenate([xd0[lo:hi, at], xd1[lo:hi, at]], axis=1)
            dy2 = dyb[lo:hi, at]
            dy4 = jnp.concatenate([dy2, dy2], axis=1)
            out = []
            for k, h in enumerate((2 * pair, 2 * pair + 1)):
                decay = jnp.exp(rowsum[h : h + 1, lo:hi] - cols[lo:hi, h : h + 1] + mt)
                out.append(mm(low(decay * gt), dy2))
                mine = wide_side if k == 0 else jnp.logical_not(wide_side)
                dw = mmt(jnp.where(mine, x2, jnp.zeros_like(x2)), dy4) * decay
                dgt = dw if dgt is None else dgt + dw
            parts.append(jnp.where(side, out[0], out[1]))
        dgt_scr[c] += dgt
        dxd = jnp.concatenate(parts, axis=1) + dxs
        xcc = xc[lo:hi]
        xdf = xd[lo:hi]
        scanned = y_in[lo:hi] - skip * xcc
        dcum_scr[lo:hi] += gather_heads(
            dyb[lo:hi].astype(f32) * scanned - xdf * dxd, group, own
        )
        tail = jnp.sum(xdf * dxs, axis=0, keepdims=True) + fx[hi - 1 : hi] * jnp.sum(
            ds * states[c], axis=0, keepdims=True
        )
        tail8 = gather_heads(jnp.broadcast_to(tail, (8, width)), group, own)
        lastrow = (iota((8, LANES), 0) == 7).astype(f32)
        dcum_scr[hi - 8 : hi] += tail8 * lastrow
        ddt_scr[lo:hi] += gather_heads(xcc * dxd, group, own)
        dxc_scr[lo:hi] = dtx[lo:hi] * dxd + skip * dy[lo:hi]
        ds = fx[hi - 1 : hi] * ds + mm3(ct[:, lo:hi], fdy[lo:hi])
    du = dxc_scr[...] * (sg + xc * (1.0 - sg))
    sums, bias = conv_back(du, xin[...], prm[0], keep, rows, taps_n, dx_scr)
    g_skip = jnp.sum(dy * xc, axis=0, keepdims=True)
    for j in range(taps_n):
        g_prm[0, j : j + 1] = sums[j]
    g_prm[0, taps_n : taps_n + 1] = bias
    g_prm[0, 5:6] = jnp.zeros_like(bias)
    g_prm[0, 6:7] = g_skip
    g_prm[0, 7:8] = jnp.zeros_like(bias)
    dxb = low(dx_scr[...])
    g_x[...] = low(mm(nrmt[...], dxb)).reshape(g_x.shape)
    part = mmt(dxb[: rows + HALO], w[...].reshape(-1, width))

    @pl.when(group == 0)
    def _():
        dn[...] = part

    @pl.when(group > 0)
    def _():
        dn[...] += part

    @pl.when(group == pl.num_programs(0) - 1)
    def _():
        half = cbc.shape[1] // 2
        dact = []
        for c in range(chunks):
            lo, hi = c * SPAN, (c + 1) * SPAN
            dgt = dgt_scr[c]
            db_scr[lo:hi] += mm3(dgt, c_in[lo:hi])
            dc_scr[lo:hi] += mm3(dgt.T, b_in[lo:hi])
        sh = shared[:, : 2 * half]
        ubc = conv(sh, cbc[...], keep, rows, taps_n)
        sgb = jax.nn.sigmoid(ubc)
        dact = jnp.concatenate([db_scr[...], dc_scr[...]], axis=1)
        dub = dact * (sgb + ubc * sgb * (1.0 - sgb))
        bsums, bbias = conv_back(dub, sh, cbc[...], keep, rows, taps_n, dbc_scr)
        for j in range(taps_n):
            g_cbc[j : j + 1] = bsums[j]
        g_cbc[taps_n : taps_n + 1] = bbias
        g_cbc[taps_n + 1 :] = jnp.zeros_like(g_cbc[taps_n + 1 :])
        raw = dtp[...]
        dt = jnp.maximum(raw, 0.0) + jnp.log1p(jnp.exp(-jnp.abs(raw)))
        upper = triangle(SPAN, False)
        for c in range(chunks):
            lo, hi = c * SPAN, (c + 1) * SPAN
            dcum_scr[lo:hi] = mmf(upper, dcum_scr[lo:hi])
        da = dcum_scr[...]
        rate = hp[1:2]
        first = iota((rows, LANES), 1) < heads
        ddtp = jnp.where(first, (rate * da + ddt_scr[...]) * jax.nn.sigmoid(raw), 0.0)
        g_hp[...] = jnp.zeros_like(g_hp)
        g_hp[0:1] = jnp.sum(ddtp, axis=0, keepdims=True)
        g_hp[1:2] = jnp.sum(jnp.where(first, da * dt * rate, 0.0), axis=0, keepdims=True)
        dsh = low(
            jnp.concatenate(
                [dbc_scr[...], jnp.concatenate([ddtp, jnp.zeros((LANES, LANES), f32)], axis=0)],
                axis=1,
            )
        )
        g_b[...] = mm(nrmt[...], dsh)
        dn[...] += mmt(dsh[: rows + HALO], wb[...])


def whole(shape):
    return pl.BlockSpec(shape, lambda g: (0,) * len(shape))


def by_column(rows, width):
    return pl.BlockSpec((rows, width), lambda g: (0, g))


def kind_block(weights, kind):
    shape = weights.shape
    return pl.BlockSpec((None, shape[1], None, shape[3], shape[4]), lambda g: (g, 0, kind, 0, 0))


def params(flops, moved):
    return dict(
        compiler_params=pltpu.CompilerParams(vmem_limit_bytes=VMEM),
        cost_estimate=pl.CostEstimate(flops=flops, bytes_accessed=moved, transcendentals=0),
    )


def struct(*shape, dtype=f32):
    return jax.ShapeDtypeStruct(shape, dtype)


def shift(x, axis, step):
    size = lax.axis_size(axis)
    return lax.ppermute(
        x, axis, [(i, i + step) for i in range(size) if 0 <= i + step < size]
    )


def bits_of(axis):
    return [(axis, b) for b in range(lax.axis_size(axis).bit_length() - 1)]


def exchange(x, axis, bit):
    return lax.ppermute(x, axis, [(i, i ^ (1 << bit)) for i in range(lax.axis_size(axis))])


def all_sum(x, order):
    for axis, bit in order:
        x = x + exchange(x, axis, bit)
    return x


def scatter_sum(x, axes, order, kind):
    names = [pair for axis in axes for pair in reversed(bits_of(axis))]
    x = x.reshape((2,) * len(names) + x.shape[len(axes) :])
    for n, (axis, bit) in enumerate(order):
        dim = names.index((axis, bit))
        mine = (lax.axis_index(axis) >> bit) & 1
        got = exchange(lax.dynamic_index_in_dim(x, 1 - mine, dim, False), axis, bit)
        x = lax.dynamic_index_in_dim(x, mine, dim, False).astype(f32) + got.astype(f32)
        if n + 1 < len(order):
            x = x.astype(kind)
        names.pop(dim)
    return x


def carry_states(state, factor, axis, backward):
    size, at = lax.axis_size(axis), lax.axis_index(axis)
    total = state.astype(f32)
    prefix = jnp.zeros_like(total)
    prefix_factor = jnp.ones_like(factor)
    step = 1
    while step < size:
        first = low(factor)
        second = low(factor - first.astype(f32))
        packed = jnp.concatenate(
            [low(total), first, second, jnp.zeros((14, factor.shape[1]), bf16)], axis=0
        )
        upper = ((at // step) % 2) == 1
        follows = jnp.logical_not(upper) if backward else upper
        pairs = [(i, i ^ step) for i in range(size)]
        final = 2 * step >= size
        if final:
            pairs = [p for p in pairs if (p[0] > p[1]) == backward]
        got = lax.ppermute(packed, axis, pairs)
        other = got[: state.shape[0]].astype(f32)
        other_factor = got[state.shape[0] : state.shape[0] + 1].astype(f32) + got[
            state.shape[0] + 1 : state.shape[0] + 2
        ].astype(f32)
        prefix = jnp.where(follows, prefix_factor * other + prefix, prefix)
        if not final:
            prefix_factor = jnp.where(follows, prefix_factor * other_factor, prefix_factor)
            total = jnp.where(follows, factor * other + total, other_factor * total + other)
            factor = factor * other_factor
        step *= 2
    return low(prefix)


def body(
    hidden,
    segment_ids,
    in_gain,
    w_zx,
    w_bcdt,
    w_out,
    conv_x,
    conv_x_bias,
    conv_bc,
    conv_bc_bias,
    dt_bias,
    a_log,
    d_skip,
    out_gain,
    cotangent,
):
    layers, taps_n = conv_x.shape[0], conv_x.shape[1]
    groups, shards = lax.axis_size("tensor"), lax.axis_size("dp")
    at_t = lax.axis_index("tensor")
    at_d = lax.axis_index("dp")
    own = dt_bias.shape[1]
    heads = own * groups
    width = out_gain.shape[1]
    full = width * groups
    rows, model = hidden.shape
    bc = conv_bc.shape[2]
    state_n = bc // 2
    depth = w_zx.shape[1]
    ext = rows + HALO
    chunks = rows // SPAN
    wide = bc + LANES
    copies = LANES // heads

    padded = jnp.pad(segment_ids.reshape(-1), (HALO, 0), constant_values=-1)
    seg = lax.dynamic_slice_in_dim(padded, at_t * rows, ext).astype(f32)
    segc = seg[:, None]
    segr = jnp.broadcast_to(seg[None, HALO:], (8, rows))

    heads_row = jnp.pad(
        jnp.concatenate([dt_bias, a_log, d_skip], axis=1), ((0, 0), (0, width - 3 * own))
    )
    pack = jnp.concatenate(
        [
            conv_x,
            conv_x_bias[:, None],
            out_gain[:, None],
            heads_row[:, None],
            jnp.zeros((layers, 1, width), f32),
        ],
        axis=1,
    )
    prm = lax.all_gather(pack, "tensor", axis=0, tiled=False)
    by_head = prm[:, :, 6]
    dtb = jnp.moveaxis(by_head[:, :, :own], 0, 1).reshape(layers, heads)
    alog = jnp.moveaxis(by_head[:, :, own : 2 * own], 0, 1).reshape(layers, heads)
    skip_ch = jnp.repeat(by_head[:, :, 2 * own : 3 * own], width // own, axis=2)
    prm = jnp.concatenate([prm[:, :, :6], skip_ch[:, :, None], prm[:, :, 7:]], axis=2)
    rate = -jnp.exp(alog)
    hp = jnp.concatenate(
        [
            jnp.tile(dtb, (1, copies))[:, None],
            jnp.tile(rate, (1, copies))[:, None],
            jnp.zeros((layers, 6, LANES), f32),
        ],
        axis=1,
    )
    cbc = jnp.concatenate(
        [conv_bc, conv_bc_bias[:, None], jnp.zeros((layers, 3, bc), f32)], axis=1
    )

    gains = lax.all_gather(in_gain, "dp", axis=1, tiled=True).astype(f32)
    weights, wbs = [], []
    for i in range(layers):
        local = jnp.concatenate(
            [jnp.moveaxis(w_zx[i], 1, 0), w_out[i][None]], axis=0
        )
        got = lax.all_gather(local, ("tensor", "dp"), axis=0, tiled=False)
        weights.append(got.reshape(groups, shards, 3, depth, width))
        wb = lax.all_gather(w_bcdt[i], "dp", axis=0, tiled=True)
        wbs.append(jnp.concatenate([wb[:, :bc], jnp.tile(wb[:, bc:], (1, copies))], axis=1))

    small = [
        ((ext, wide), f32),
        ((rows, state_n), f32),
        ((rows, state_n), f32),
        ((state_n, rows), f32),
        ((state_n, rows), f32),
        ((rows, LANES), f32),
        ((LANES, rows), f32),
        ((rows, LANES), bf16),
        ((rows, LANES), bf16),
        ((rows, LANES), bf16),
        ((rows, LANES), bf16),
        ((rows, LANES), bf16),
    ]
    prm_spec = pl.BlockSpec((1, 8, width), lambda g: (g, 0, 0))
    saved = []
    stream = hidden
    for i in range(layers):
        rinv = lax.rsqrt(jnp.mean(stream * stream, axis=-1, keepdims=True) + epsilon)
        normed = (stream * rinv * gains[i]).astype(bf16)
        before = shift(normed[rows - HALO :], "tensor", 1)
        nrm = jnp.concatenate([before, normed], axis=0)
        nrmt = jnp.concatenate(
            [normed, before, jnp.zeros((LANES - HALO, model), bf16)], axis=0
        ).T
        w, wb, pr = weights[i], wbs[i], prm[:, i]
        flops = 2 * ext * model * (full + wide)
        outs = pl.pallas_call(
            partial(scan_in_kernel, heads, own, taps_n),
            grid=(groups,),
            in_specs=[
                whole((ext, model)),
                kind_block(w, 1),
                whole((model, wide)),
                prm_spec,
                whole((8, bc)),
                whole((8, LANES)),
                whole((ext, 1)),
                whole((8, rows)),
            ],
            out_specs=[
                by_column(rows, width),
                by_column(ext, width),
                by_column(state_n, width),
                by_column(8, width),
            ]
            + [whole(s) for s, _ in small],
            out_shape=[
                struct(rows, full),
                struct(ext, full),
                struct(state_n, full, dtype=bf16),
                struct(8, full),
            ]
            + [struct(*s, dtype=d) for s, d in small],
            scratch_shapes=[
                pltpu.VMEM((chunks, SPAN, SPAN), f32),
                pltpu.VMEM((chunks, SPAN, SPAN), f32),
            ],
            name="scan_in",
            **params(3 * flops, 4 * rows * full * 3),
        )(nrm, w, wb, pr, cbc[i], hp[i], segc, segr)
        y_loc, xin, state, ftot = outs[:4]
        rest = outs[4:]
        shared, b_m, c_m, b_t, c_t, dtp, cumt, dts, es, fs, fd, cums = rest
        s_in = carry_states(state, ftot[0:1], "tensor", False)
        z, y, branch, grms, nxt = pl.pallas_call(
            partial(gate_kernel, heads, own, full),
            grid=(groups,),
            in_specs=[
                whole((ext, model)),
                kind_block(w, 0),
                kind_block(w, 2),
                by_column(rows, width),
                whole((rows, state_n)),
                whole((rows, LANES)),
                by_column(state_n, width),
                prm_spec,
                whole((rows, model)),
            ],
            out_specs=[
                by_column(rows, width),
                by_column(rows, width),
                whole((rows, model)),
                whole((rows, LANES)),
                whole((rows, model)),
            ],
            out_shape=[
                struct(rows, full),
                struct(rows, full),
                struct(rows, model),
                struct(rows, LANES),
                struct(rows, model),
            ],
            scratch_shapes=[pltpu.VMEM((rows, LANES), f32)],
            name="gate",
            **params(4 * rows * model * full, 4 * rows * full * 5),
        )(nrm, w, w, y_loc, c_m, fd, s_in, pr, stream)
        saved.append((stream, rinv, nrmt, xin, ftot, rest, s_in, z, y, branch, grms))
        stream = nxt

    grad = cotangent
    big, shared_grads, gain_grads, prm_grads, cbc_grads, hp_grads = [], [], [], [], [], []
    in_gain_grads = []
    tb, db = bits_of("tensor"), bits_of("dp")
    order_x = tb + db
    order_y = tb[:1] + db[:1] + tb[1:] + db[1:]
    for i in reversed(range(layers)):
        stream_in, rinv, nrmt, xin, ftot, rest, s_in, z, y, branch, grms = saved[i]
        shared, b_m, c_m, b_t, c_t, dtp, cumt, dts, es, fs, fd, cums = rest
        w, wb, pr = weights[i], wbs[i], prm[:, i]
        dbr = grad.astype(bf16)
        grad_block = pl.BlockSpec((None, shards, depth, width), lambda g: (g, 0, 0, 0))
        grad_shape = struct(groups, shards, depth, width, dtype=bf16)
        g_out, g_z, dy, dnz, dstate, g_gain = pl.pallas_call(
            partial(gate_back_kernel, heads, own, full),
            grid=(groups,),
            in_specs=[
                whole((rows, model)),
                whole((model, rows)),
                whole((rows, model)),
                kind_block(w, 2),
                kind_block(w, 0),
                by_column(rows, width),
                by_column(rows, width),
                whole((rows, LANES)),
                whole((model, rows + LANES)),
                whole((state_n, rows)),
                whole((rows, LANES)),
                prm_spec,
            ],
            out_specs=[
                grad_block,
                grad_block,
                by_column(rows, width),
                whole((rows, model)),
                by_column(state_n, width),
                by_column(8, width),
            ],
            out_shape=[
                grad_shape,
                grad_shape,
                struct(rows, full),
                struct(rows, model),
                struct(state_n, full, dtype=bf16),
                struct(8, full),
            ],
            scratch_shapes=[pltpu.VMEM((rows, LANES), f32)],
            name="gate_back",
            **params(8 * rows * model * full, 4 * rows * full * 6),
        )(dbr, dbr.T, branch, w, w, z, y, grms, nrmt, c_t, fd, pr)
        ds_in = carry_states(dstate, ftot[0:1], "tensor", True)
        g_x, g_b, dn, g_prm, g_cbc, g_hp = pl.pallas_call(
            partial(scan_back_kernel, heads, own, taps_n),
            grid=(groups,),
            in_specs=[
                by_column(ext, width),
                by_column(rows, width),
                by_column(rows, width),
                by_column(state_n, width),
                by_column(state_n, width),
                kind_block(w, 1),
                whole((model, wide)),
                prm_spec,
                whole((8, bc)),
                whole((8, LANES)),
                whole((ext, 1)),
                whole((8, rows)),
                whole((model, rows + LANES)),
            ]
            + [whole(s) for n, (s, _) in enumerate(small) if n != 10],
            out_specs=[
                grad_block,
                whole((model, wide)),
                whole((ext, model)),
                pl.BlockSpec((1, 8, width), lambda g: (g, 0, 0)),
                whole((8, bc)),
                whole((8, LANES)),
            ],
            out_shape=[
                grad_shape,
                struct(model, wide),
                struct(ext, model),
                struct(groups, 8, width),
                struct(8, bc),
                struct(8, LANES),
            ],
            scratch_shapes=[
                pltpu.VMEM((chunks, SPAN, SPAN), f32),
                pltpu.VMEM((chunks, SPAN, SPAN), f32),
                pltpu.VMEM((chunks, SPAN, SPAN), f32),
                pltpu.VMEM((rows, state_n), f32),
                pltpu.VMEM((rows, state_n), f32),
                pltpu.VMEM((rows, LANES), f32),
                pltpu.VMEM((rows, LANES), f32),
                pltpu.VMEM((rows + LANES, width), f32),
                pltpu.VMEM((rows + LANES, bc), f32),
                pltpu.VMEM((rows, width), f32),
            ],
            name="scan_back",
            **params(8 * rows * model * full, 4 * rows * full * 6),
        )(
            xin, dy, y, s_in, ds_in, w, wb, pr, cbc[i], hp[i], segc, segr, nrmt,
            shared, b_m, c_m, b_t, c_t, dtp, cumt, dts, es, fs, cums,
        )
        after = shift(dn[rows:], "tensor", -1)
        dnormed = dnz + dn[:rows]
        dnormed = jnp.concatenate(
            [dnormed[: rows - HALO], dnormed[rows - HALO :] + after], axis=0
        )
        scaled_in = stream_in * rinv
        gain_grads.append(jnp.sum(dnormed * scaled_in, axis=0))
        scaled = dnormed * gains[i]
        grad = grad + rinv * (
            scaled - scaled_in * jnp.mean(scaled * scaled_in, axis=-1, keepdims=True)
        )

        rows_b = depth // groups
        parts_b = jnp.pad(
            low(g_b[:, : bc + heads]), ((0, 0), (0, wide - bc - heads))
        ).reshape(shards, groups, rows_b * wide // width, width)
        with_b = jnp.concatenate([g_x, jnp.moveaxis(parts_b, 1, 0)], axis=2)
        half = width // 2
        left = scatter_sum(with_b[..., :half], ("tensor", "dp"), order_x, bf16)
        right = scatter_sum(with_b[..., half:], ("tensor", "dp"), order_y, bf16)
        with_b = jnp.concatenate([left, right], axis=1)
        big.append(
            (
                scatter_sum(g_z, ("tensor", "dp"), order_x, bf16),
                with_b[:depth],
                scatter_sum(g_out, ("tensor", "dp"), order_y, bf16),
            )
        )
        shared_grads.append(with_b[depth:].reshape(rows_b, wide)[:, : bc + heads])
        g_prm = g_prm.at[:, 5].set(g_gain[0].reshape(groups, width))
        g_prm = scatter_sum(g_prm, ("tensor",), bits_of("tensor"), f32)
        rest_sum = jnp.concatenate([gain_grads[-1], g_cbc.reshape(-1), g_hp.reshape(-1)])
        rest_sum = all_sum(rest_sum.reshape(-1, width), bits_of("tensor"))
        rest_sum = all_sum(jnp.concatenate([g_prm, rest_sum], axis=0), bits_of("dp"))
        prm_grads.append(rest_sum[:8])
        rest_sum = rest_sum[8:].reshape(-1)
        gain_all = rest_sum[:model]
        cbc_grads.append(rest_sum[model : model + 8 * bc].reshape(8, bc))
        hp_grads.append(rest_sum[model + 8 * bc :].reshape(8, LANES))
        per = model // (groups * shards)
        in_gain_grads.append(
            lax.dynamic_slice_in_dim(gain_all, (at_d * groups + at_t) * per, per, 0)
        )

    def stacked(items):
        return jnp.stack(items[::-1], axis=0)

    grad_w_zx = jnp.stack([stacked([b[0] for b in big]), stacked([b[1] for b in big])], axis=2)
    grad_w_out = stacked([b[2] for b in big])
    grad_w_bcdt = stacked(shared_grads)
    grad_in_gain = stacked(in_gain_grads)
    mine = stacked(prm_grads)
    cbc_all = stacked(cbc_grads)
    hp_all = stacked(hp_grads)
    heads_mine = lax.dynamic_slice_in_dim(hp_all, at_t * own, own, 2)
    return (
        stream,
        grad,
        grad_in_gain,
        grad_w_zx,
        grad_w_bcdt,
        grad_w_out,
        mine[:, :taps_n],
        mine[:, taps_n],
        cbc_all[:, :taps_n],
        cbc_all[:, taps_n],
        heads_mine[:, 0],
        heads_mine[:, 1],
        mine[:, 6].reshape(layers, own, width // own).sum(axis=-1),
        mine[:, 5],
    )


def solution(mesh):
    placed = (
        P(("dp", "tensor"), None),
        P("dp", None),
        P(None, "dp"),
        P(None, "dp", None, "tensor"),
        P(None, "dp", None),
        P(None, "dp", "tensor"),
        P(None, None, "tensor"),
        P(None, "tensor"),
        P(),
        P(),
        P(None, "tensor"),
        P(None, "tensor"),
        P(None, "tensor"),
        P(None, "tensor"),
        P(("dp", "tensor"), None),
    )
    return jax.shard_map(
        body,
        mesh=mesh,
        in_specs=placed,
        out_specs=(
            P(("dp", "tensor"), None),
            P(("dp", "tensor"), None),
            P(None, ("dp", "tensor")),
            P(None, "dp", None, "tensor"),
            P(None, ("dp", "tensor"), None),
            P(None, "dp", "tensor"),
            P(None, None, "tensor"),
            P(None, "tensor"),
            P(),
            P(),
            P(None, "tensor"),
            P(None, "tensor"),
            P(None, "tensor"),
            P(None, "tensor"),
        ),
        check_vma=False,
    )
```

```python
from functools import partial

import jax
import jax.numpy as jnp
from jax import lax
from jax.experimental import pallas as pl
from jax.experimental.pallas import tpu as pltpu
from jax.sharding import PartitionSpec as P

bf16 = jnp.bfloat16
f32 = jnp.float32
epsilon = 1e-05
SPAN = 256
HALO = 16
LANES = 128
NEG = -1e30
VMEM = 56 * 1024 * 1024


def mm(a, b):
    return lax.dot_general(a, b, (((1,), (0,)), ((), ())), preferred_element_type=f32)


def mmt(a, b):
    return lax.dot_general(a, b, (((1,), (1,)), ((), ())), preferred_element_type=f32)


def mmf(a, b):
    return lax.dot_general(
        a, b, (((1,), (0,)), ((), ())), precision=lax.Precision.HIGHEST, preferred_element_type=f32
    )


def two(x):
    first = low(x)
    return first, low(x - first.astype(f32))


def mm3(a, b):
    a0, a1 = two(a)
    b0, b1 = two(b)
    return mm(a0, b0) + (mm(a0, b1) + mm(a1, b0))


def mmt3(a, b):
    a0, a1 = two(a)
    b0, b1 = two(b)
    return mmt(a0, b0) + (mmt(a0, b1) + mmt(a1, b0))


def iota(shape, axis):
    return lax.broadcasted_iota(jnp.int32, shape, axis)


def low(x):
    return x.astype(bf16)


def three(x):
    first = low(x).astype(f32)
    rest = x - first
    second = low(rest).astype(f32)
    return first, second, rest - second


def split_heads(x, heads):
    first, second, third = three(x)
    part = iota(x.shape, 1) // heads
    zero = jnp.zeros_like(x)
    return low(
        jnp.where(part == 0, first, jnp.where(part == 1, second, jnp.where(part == 2, third, zero)))
    )


def spread(group, heads, own, width):
    row, col = iota((LANES, width), 0), iota((LANES, width), 1)
    return low(
        ((row % heads == group * own + col // (width // own)) & (row < 3 * heads)).astype(f32)
    )


def pick(group, heads, own):
    row, col = iota((LANES, LANES), 0), iota((LANES, LANES), 1)
    return low(((row % heads == group * own + col) & (col < own) & (row < 3 * heads)).astype(f32))


def gather_heads(x, group, own):
    width = x.shape[1]
    row, col = iota((width, LANES), 0), iota((width, LANES), 1)
    fold = low((col == group * own + row // (width // own)).astype(f32))
    first, second, third = three(x)
    return mm(low(first), fold) + mm(low(second), fold) + mm(low(third), fold)


def keeps(segc, rows):
    now = segc[HALO : HALO + rows]
    return [None] + [
        (segc[HALO - j : HALO - j + rows] == now).astype(f32) for j in range(1, 4)
    ]


def conv(ext, taps, keep, rows, count):
    total = taps[count : count + 1] + taps[0:1] * ext[HALO : HALO + rows]
    for j in range(1, count):
        total = total + taps[j : j + 1] * (ext[HALO - j : HALO - j + rows] * keep[j])
    return total


def triangle(rows, lower):
    row, col = iota((rows, rows), 0), iota((rows, rows), 1)
    return ((row >= col) if lower else (row <= col)).astype(f32)


def scan_in_kernel(heads, own, taps_n, pieces, nrm, *refs):
    w, refs = refs[:pieces], refs[pieces:]
    (
        wb,
        prm,
        cbc,
        hp,
        segc,
        segr,
        y,
        xin,
        state,
        ftot,
        shared,
        b_out,
        c_out,
        bt_out,
        ct_out,
        dtp_out,
        cumt_out,
        dts_out,
        es_out,
        fs_out,
        fd_out,
        cums_out,
        g_scr,
        m_scr,
    ) = refs
    group = pl.program_id(0)
    rows = y.shape[0]
    width = y.shape[1]
    chunks = rows // SPAN
    keep = keeps(segc[...], rows)

    @pl.when(group == 0)
    def _():
        sh = mm(nrm[...], wb[...])
        shared[...] = sh
        half = cbc.shape[1] // 2
        act = conv(sh[:, : 2 * half], cbc[...], keep, rows, taps_n)
        act = act * jax.nn.sigmoid(act)
        bmat, cmat = act[:, :half], act[:, half:]
        b_out[...] = bmat
        c_out[...] = cmat
        bt_out[...] = bmat.T
        ct_out[...] = cmat.T
        dtp = sh[HALO:, 2 * half :] + hp[0:1]
        dtp_out[...] = dtp
        dt = jnp.maximum(dtp, 0.0) + jnp.log1p(jnp.exp(-jnp.abs(dtp)))
        cum = mmf(triangle(rows, True), dt * hp[1:2])
        cumt_out[...] = cum.T
        dts_out[...] = split_heads(dt, heads)
        cums_out[...] = split_heads(cum, heads)
        seg = segc[...]
        here = seg[HALO:]
        fd_out[...] = split_heads(
            jnp.exp(cum) * (here == seg[HALO - 1 : HALO]).astype(f32), heads
        )
        for c in range(chunks):
            lo, hi = c * SPAN, (c + 1) * SPAN
            block = cum[lo:hi]
            base = jnp.zeros_like(cum[0:1]) if c == 0 else cum[lo - 1 : lo]
            before = seg[HALO + lo - 1 : HALO + lo]
            last = here[hi - 1 : hi]
            fs_out[lo:hi] = split_heads(
                jnp.exp(block - base) * (here[lo:hi] == before).astype(f32), heads
            )
            es_out[lo:hi] = split_heads(
                jnp.exp(cum[hi - 1 : hi] - block) * (here[lo:hi] == last).astype(f32), heads
            )
            g_scr[c] = mmt3(cmat[lo:hi], bmat[lo:hi])
            ok = (here[lo:hi] == segr[0:1, lo:hi]) & (
                iota((SPAN, SPAN), 0) >= iota((SPAN, SPAN), 1)
            )
            m_scr[c] = jnp.where(ok, 0.0, NEG)

    ext = jnp.concatenate(
        [mm(nrm[...], part[...].reshape(nrm.shape[1], -1)) for part in w], axis=1
    )
    xin[...] = ext
    u = conv(ext, prm[0], keep, rows, taps_n)
    xc = u * jax.nn.sigmoid(u)
    grow = spread(group, heads, own, width)
    xd = xc * mm(dts_out[...], grow)
    xd0, xd1 = two(xd)
    exd = xd * mm(es_out[...], grow)
    fx = mm(fs_out[...], grow)
    cols = mm(cums_out[...], pick(group, heads, own))
    rowsum = cumt_out[pl.ds(pl.multiple_of(group * own, own), own), :]
    per = width // own
    side = iota((SPAN, 2 * per), 1) < per
    now = None
    for c in range(chunks):
        lo, hi = c * SPAN, (c + 1) * SPAN
        m, g = m_scr[c], g_scr[c]
        for pair in range(own // 2):
            at = slice(2 * per * pair, 2 * per * (pair + 1))
            x2 = jnp.concatenate([xd0[lo:hi, at], xd1[lo:hi, at]], axis=1)
            out = []
            for h in (2 * pair, 2 * pair + 1):
                decay = jnp.exp(cols[lo:hi, h : h + 1] - rowsum[h : h + 1, lo:hi] + m)
                both = mm(low(decay * g), x2)
                out.append(both[:, : 2 * per] + both[:, 2 * per :])
            y[lo:hi, at] = (
                jnp.where(side, out[0], out[1]) + prm[0, 6:7, at] * xc[lo:hi, at]
            )
        local = mm3(bt_out[:, lo:hi], exd[lo:hi])
        if c > 0:
            y[lo:hi] += fx[lo:hi] * mm3(c_out[lo:hi], now)
            now = fx[hi - 1 : hi] * now + local
        else:
            now = local
    whole_factor = mm(fd_out[...], grow)[rows - 1 : rows]
    ftot[...] = jnp.broadcast_to(whole_factor, ftot.shape)
    put_state(state, now, whole_factor)


def gate_kernel(
    heads,
    own,
    full,
    nrm,
    wz,
    wo,
    y_loc,
    c_in,
    fd,
    s_in,
    prm,
    hid,
    z_out,
    y_out,
    branch,
    grms,
    nxt,
    ss,
    gated_scr,
):
    group = pl.program_id(0)
    width = y_loc.shape[1]
    z = mm(nrm[HALO:], wz[...].reshape(-1, width))
    y = y_loc[...] + mm(fd[...], spread(group, heads, own, width)) * (
        lambda parts: mm(parts[0], s_in[...]) + mm(parts[1], s_in[...])
    )(two(c_in[...]))
    z_out[...] = z
    y_out[...] = y
    gated = y * (z * jax.nn.sigmoid(z))
    squares = jnp.sum(gated * gated, axis=1, keepdims=True)
    gated_scr[group] = gated

    @pl.when(group == 0)
    def _():
        ss[...] = jnp.broadcast_to(squares, ss.shape)

    @pl.when(group > 0)
    def _():
        ss[...] += jnp.broadcast_to(squares, ss.shape)

    @pl.when(group == pl.num_programs(0) - 1)
    def _():
        scale = lax.rsqrt(ss[...] / full + epsilon)
        grms[...] = scale
        total = None
        for g in range(prm.shape[0]):
            mixed = low(gated_scr[g] * scale[:, 0:1] * prm[g, 5:6])
            part = mmt(mixed, wo[g].reshape(-1, width))
            total = part if total is None else total + part
        branch[...] = total
        nxt[...] = hid[...] + total


def gate_back_kernel(
    heads,
    own,
    full,
    dbr,
    dbrt,
    branch,
    wo,
    wz,
    z_in,
    y_in,
    grms,
    nrmt,
    ct,
    fd,
    prm,
    g_zo,
    dy_out,
    dn,
    dstate,
    g_gain,
    q_scr,
):
    group = pl.program_id(0)
    rows, width = z_in.shape
    depth = wz.shape[1]
    block = wz.shape

    @pl.when(group == 0)
    def _():
        inner = jnp.sum(dbr[...].astype(f32) * branch[...], axis=1, keepdims=True)
        q_scr[...] = grms[...] * grms[...] * (inner / full)

    rms = grms[:, 0:1]
    dm = mm(dbr[...], wo[...].reshape(-1, width))
    z, y = z_in[...], y_in[...]
    sg = jax.nn.sigmoid(z)
    sz = z * sg
    gated = y * sz
    scaled = gated * rms
    gain = prm[0, 5:6]
    g_zo[:, depth:] = low(mm(dbrt[...], low(scaled * gain))).reshape(block)
    g_gain[...] = jnp.broadcast_to(jnp.sum(dm * scaled, axis=0, keepdims=True), g_gain.shape)
    dg = rms * (dm * gain) - gated * q_scr[:, 0:1]
    dy = dg * sz
    dy_out[...] = dy
    dz = low(dg * y * (sg + sz * (1.0 - sg)))
    g_zo[:, :depth] = low(mm(nrmt[:, :rows], dz)).reshape(block)
    part = mmt(dz, wz[...].reshape(-1, width))

    @pl.when(group == 0)
    def _():
        dn[...] = part

    @pl.when(group > 0)
    def _():
        dn[...] += part

    fx = mm(fd[...], spread(group, heads, own, width))
    put_state(dstate, mm3(ct[...], fx * dy), fx[rows - 1 : rows])


def put_state(state, now, factor):
    high, rest = two(factor)
    count = state.shape[0] - now.shape[0]
    row = iota((count, factor.shape[1]), 0)
    tail = jnp.where(row == 0, high.astype(f32), jnp.where(row == 1, rest.astype(f32), 0.0))
    state[...] = low(jnp.concatenate([now, tail], axis=0))


def conv_back(du, ext, taps, keep, rows, count, dest):
    dest[...] = jnp.zeros_like(dest)
    dest[0:rows] = taps[0:1] * du
    sums = [jnp.sum(du * ext[HALO : HALO + rows], axis=0, keepdims=True)]
    for j in range(1, count):
        kept = du * keep[j]
        sums.append(jnp.sum(kept * ext[HALO - j : HALO - j + rows], axis=0, keepdims=True))
        moved = taps[j : j + 1] * kept
        dest[0 : rows - j] += moved[j:]
        dest[rows + HALO - j : rows + HALO] += moved[:j]
    return sums, jnp.sum(du, axis=0, keepdims=True)


def scan_back_kernel(heads, own, taps_n, pieces, xin, dy_in, y_in, s_in, ds_in, *refs):
    w, refs = refs[:pieces], refs[pieces:]
    (
        wb,
        prm,
        cbc,
        hp,
        segc,
        segr,
        nrmt,
        shared,
        b_in,
        c_in,
        bt,
        ct,
        dtp,
        cumt,
        dts,
        es,
        fs,
        cums,
        g_x,
        g_b,
        dn,
        g_prm,
        g_cbc,
        g_hp,
        gt_scr,
        mt_scr,
        dgt_scr,
        db_scr,
        dc_scr,
        dcum_scr,
        ddt_scr,
        dx_scr,
        dbc_scr,
        dxc_scr,
    ) = refs
    group = pl.program_id(0)
    rows, width = dy_in.shape
    chunks = rows // SPAN
    keep = keeps(segc[...], rows)

    @pl.when(group == 0)
    def _():
        here = segc[HALO:]
        for c in range(chunks):
            lo, hi = c * SPAN, (c + 1) * SPAN
            gt_scr[c] = mmt3(b_in[lo:hi], c_in[lo:hi])
            ok = (here[lo:hi] == segr[0:1, lo:hi]) & (
                iota((SPAN, SPAN), 0) <= iota((SPAN, SPAN), 1)
            )
            mt_scr[c] = jnp.where(ok, 0.0, NEG)
        for ref in (dgt_scr, db_scr, dc_scr, dcum_scr, ddt_scr):
            ref[...] = jnp.zeros_like(ref)

    u = conv(xin[...], prm[0], keep, rows, taps_n)
    sg = jax.nn.sigmoid(u)
    xc = u * sg
    grow = spread(group, heads, own, width)
    dtx = mm(dts[...], grow)
    ex = mm(es[...], grow)
    fx = mm(fs[...], grow)
    xd = xc * dtx
    xd0, xd1 = two(xd)
    exd = xd * ex
    cols = mm(cums[...], pick(group, heads, own))
    rowsum = cumt[pl.ds(pl.multiple_of(group * own, own), own), :]
    dy = dy_in[...]
    dyb = low(dy)
    fdy = fx * dy
    skip = prm[0, 6:7]
    per = width // own
    side = iota((SPAN, 2 * per), 1) < per
    wide_side = (iota((SPAN, 4 * per), 1) // per) % 2 == 0
    states = [s_in[...].astype(f32)]
    for c in range(chunks - 1):
        lo, hi = c * SPAN, (c + 1) * SPAN
        states.append(fx[hi - 1 : hi] * states[-1] + mm3(bt[:, lo:hi], exd[lo:hi]))
    ds = ds_in[...].astype(f32)
    for c in reversed(range(chunks)):
        lo, hi = c * SPAN, (c + 1) * SPAN
        dxs = ex[lo:hi] * mm3(b_in[lo:hi], ds)
        db_scr[lo:hi] += mmt3(exd[lo:hi], ds)
        dc_scr[lo:hi] += mmt3(fdy[lo:hi], states[c])
        mt, gt = mt_scr[c], gt_scr[c]
        parts = []
        dgt = None
        for pair in range(own // 2):
            at = slice(2 * per * pair, 2 * per * (pair + 1))
            x2 = jnp.concatenate([xd0[lo:hi, at], xd1[lo:hi, at]], axis=1)
            dy2 = dyb[lo:hi, at]
            dy4 = jnp.concatenate([dy2, dy2], axis=1)
            out = []
            for k, h in enumerate((2 * pair, 2 * pair + 1)):
                decay = jnp.exp(rowsum[h : h + 1, lo:hi] - cols[lo:hi, h : h + 1] + mt)
                out.append(mm(low(decay * gt), dy2))
                mine = wide_side if k == 0 else jnp.logical_not(wide_side)
                dw = mmt(jnp.where(mine, x2, jnp.zeros_like(x2)), dy4) * decay
                dgt = dw if dgt is None else dgt + dw
            parts.append(jnp.where(side, out[0], out[1]))
        dgt_scr[c] += dgt
        dxd = jnp.concatenate(parts, axis=1) + dxs
        xcc = xc[lo:hi]
        xdf = xd[lo:hi]
        scanned = y_in[lo:hi] - skip * xcc
        dcum_scr[lo:hi] += gather_heads(
            dyb[lo:hi].astype(f32) * scanned - xdf * dxd, group, own
        )
        tail = jnp.sum(xdf * dxs, axis=0, keepdims=True) + fx[hi - 1 : hi] * jnp.sum(
            ds * states[c], axis=0, keepdims=True
        )
        tail8 = gather_heads(jnp.broadcast_to(tail, (8, width)), group, own)
        lastrow = (iota((8, LANES), 0) == 7).astype(f32)
        dcum_scr[hi - 8 : hi] += tail8 * lastrow
        ddt_scr[lo:hi] += gather_heads(xcc * dxd, group, own)
        dxc_scr[lo:hi] = dtx[lo:hi] * dxd + skip * dy[lo:hi]
        ds = fx[hi - 1 : hi] * ds + mm3(ct[:, lo:hi], fdy[lo:hi])
    du = dxc_scr[...] * (sg + xc * (1.0 - sg))
    sums, bias = conv_back(du, xin[...], prm[0], keep, rows, taps_n, dx_scr)
    g_skip = jnp.sum(dy * xc, axis=0, keepdims=True)
    for j in range(taps_n):
        g_prm[0, j : j + 1] = sums[j]
    g_prm[0, taps_n : taps_n + 1] = bias
    g_prm[0, 5:6] = jnp.zeros_like(bias)
    g_prm[0, 6:7] = g_skip
    g_prm[0, 7:8] = jnp.zeros_like(bias)
    dxb = low(dx_scr[...])
    g_x[...] = low(mm(nrmt[...], dxb)).reshape(g_x.shape)
    part, step = None, width // pieces
    for n, weight in enumerate(w):
        term = mmt(
            dxb[: rows + HALO, n * step : (n + 1) * step],
            weight[...].reshape(-1, step),
        )
        part = term if part is None else part + term

    @pl.when(group == 0)
    def _():
        dn[...] = part

    @pl.when(group > 0)
    def _():
        dn[...] += part

    @pl.when(group == pl.num_programs(0) - 1)
    def _():
        half = cbc.shape[1] // 2
        dact = []
        for c in range(chunks):
            lo, hi = c * SPAN, (c + 1) * SPAN
            dgt = dgt_scr[c]
            db_scr[lo:hi] += mm3(dgt, c_in[lo:hi])
            dc_scr[lo:hi] += mm3(dgt.T, b_in[lo:hi])
        sh = shared[:, : 2 * half]
        ubc = conv(sh, cbc[...], keep, rows, taps_n)
        sgb = jax.nn.sigmoid(ubc)
        dact = jnp.concatenate([db_scr[...], dc_scr[...]], axis=1)
        dub = dact * (sgb + ubc * sgb * (1.0 - sgb))
        bsums, bbias = conv_back(dub, sh, cbc[...], keep, rows, taps_n, dbc_scr)
        for j in range(taps_n):
            g_cbc[j : j + 1] = bsums[j]
        g_cbc[taps_n : taps_n + 1] = bbias
        g_cbc[taps_n + 1 :] = jnp.zeros_like(g_cbc[taps_n + 1 :])
        raw = dtp[...]
        dt = jnp.maximum(raw, 0.0) + jnp.log1p(jnp.exp(-jnp.abs(raw)))
        upper = triangle(SPAN, False)
        for c in range(chunks):
            lo, hi = c * SPAN, (c + 1) * SPAN
            dcum_scr[lo:hi] = mmf(upper, dcum_scr[lo:hi])
        da = dcum_scr[...]
        rate = hp[1:2]
        first = iota((rows, LANES), 1) < heads
        ddtp = jnp.where(first, (rate * da + ddt_scr[...]) * jax.nn.sigmoid(raw), 0.0)
        g_hp[...] = jnp.zeros_like(g_hp)
        g_hp[0:1] = jnp.sum(ddtp, axis=0, keepdims=True)
        g_hp[1:2] = jnp.sum(jnp.where(first, da * dt * rate, 0.0), axis=0, keepdims=True)
        dsh = low(
            jnp.concatenate(
                [dbc_scr[...], jnp.concatenate([ddtp, jnp.zeros((LANES, LANES), f32)], axis=0)],
                axis=1,
            )
        )
        g_b[...] = mm(nrmt[...], dsh)
        dn[...] += mmt(dsh[: rows + HALO], wb[...])


def whole(shape):
    return pl.BlockSpec(shape, lambda g: (0,) * len(shape))


def by_column(rows, width):
    return pl.BlockSpec((rows, width), lambda g: (0, g))


def kind_block(depth, pair):
    weights, kind = pair
    shape = weights.shape
    return pl.BlockSpec((None, shape[1], depth, shape[3]), lambda g: (g, 0, kind, 0))


def params(flops, moved):
    return dict(
        compiler_params=pltpu.CompilerParams(vmem_limit_bytes=VMEM),
        cost_estimate=pl.CostEstimate(flops=flops, bytes_accessed=moved, transcendentals=0),
    )


def struct(*shape, dtype=f32):
    return jax.ShapeDtypeStruct(shape, dtype)


def shift(x, axis, step):
    size = lax.axis_size(axis)
    return lax.ppermute(
        x, axis, [(i, i + step) for i in range(size) if 0 <= i + step < size]
    )


def bits_of(axis):
    return [(axis, b) for b in range(lax.axis_size(axis).bit_length() - 1)]


def exchange(x, axis, bit):
    return lax.ppermute(x, axis, [(i, i ^ (1 << bit)) for i in range(lax.axis_size(axis))])


def all_sum(x, order):
    for axis, bit in order:
        x = x + exchange(x, axis, bit)
    return x


def scatter_start(x, axes):
    names = [pair for axis in axes for pair in reversed(bits_of(axis))]
    return x.reshape((2,) * len(names) + x.shape[len(axes) :]), names


def outgoing(x, names, pair):
    axis, bit = pair
    mine = (lax.axis_index(axis) >> bit) & 1
    return lax.dynamic_index_in_dim(x, 1 - mine, names.index(pair), False)


def scatter_step(x, names, pair, got=None, kind=bf16):
    axis, bit = pair
    mine = (lax.axis_index(axis) >> bit) & 1
    if got is None:
        got = exchange(outgoing(x, names, pair), axis, bit)
    x = lax.dynamic_index_in_dim(x, mine, names.index(pair), False)
    x = (x.astype(f32) + got.astype(f32)).astype(kind)
    return x, [name for name in names if name != pair]


def scatter_rest(x, names, order, kind=bf16):
    for n, pair in enumerate(order):
        x, names = scatter_step(x, names, pair, None, f32 if n + 1 == len(order) else kind)
    return x


def carry_states(packed, axis, backward):
    size, at = lax.axis_size(axis), lax.axis_index(axis)
    count = packed.shape[0] - HALO

    def unpack(x):
        x = x.astype(f32)
        return x[:count], x[count : count + 1] + x[count + 1 : count + 2]

    total, factor = unpack(packed)
    prefix = jnp.zeros_like(total)
    prefix_factor = jnp.ones_like(factor)
    step = 1
    while step < size:
        upper = ((at // step) % 2) == 1
        follows = jnp.logical_not(upper) if backward else upper
        pairs = [(i, i ^ step) for i in range(size)]
        final = 2 * step >= size
        if final:
            pairs = [p for p in pairs if (p[0] > p[1]) == backward]
        other, other_factor = unpack(lax.ppermute(packed, axis, pairs))
        prefix = jnp.where(follows, prefix_factor * other + prefix, prefix)
        if not final:
            prefix_factor = jnp.where(follows, prefix_factor * other_factor, prefix_factor)
            total = jnp.where(follows, factor * other + total, other_factor * total + other)
            factor = factor * other_factor
            high, rest = two(factor)
            packed = jnp.concatenate(
                [low(total), high, rest, jnp.zeros((HALO - 2, factor.shape[1]), bf16)], axis=0
            )
        step *= 2
    return low(prefix)


def body(
    hidden,
    segment_ids,
    in_gain,
    w_zx,
    w_bcdt,
    w_out,
    conv_x,
    conv_x_bias,
    conv_bc,
    conv_bc_bias,
    dt_bias,
    a_log,
    d_skip,
    out_gain,
    cotangent,
):
    layers, taps_n = conv_x.shape[0], conv_x.shape[1]
    groups, shards = lax.axis_size("tensor"), lax.axis_size("dp")
    tb, db = bits_of("tensor"), bits_of("dp")
    axes = ("tensor", "dp")
    order_x = tb + db
    order_y = tb[:1] + db[:1] + tb[1:] + db[1:]
    at_t = lax.axis_index("tensor")
    at_d = lax.axis_index("dp")
    own = dt_bias.shape[1]
    heads = own * groups
    width = out_gain.shape[1]
    full = width * groups
    rows, model = hidden.shape
    bc = conv_bc.shape[2]
    state_n = bc // 2
    depth = w_zx.shape[1]
    ext = rows + HALO
    chunks = rows // SPAN
    wide = bc + LANES
    copies = LANES // heads

    padded = jnp.pad(segment_ids.reshape(-1), (HALO, 0), constant_values=-1)
    seg = lax.dynamic_slice_in_dim(padded, at_t * rows, ext).astype(f32)
    segc = seg[:, None]
    segr = jnp.broadcast_to(seg[None, HALO:], (8, rows))

    heads_row = jnp.pad(
        jnp.concatenate([dt_bias, a_log, d_skip], axis=1), ((0, 0), (0, width - 3 * own))
    )
    pack = jnp.concatenate(
        [
            conv_x,
            conv_x_bias[:, None],
            out_gain[:, None],
            heads_row[:, None],
            jnp.zeros((layers, 1, width), f32),
        ],
        axis=1,
    )
    prm = lax.all_gather(pack, "tensor", axis=0, tiled=False)
    by_head = prm[:, :, 6]
    dtb = jnp.moveaxis(by_head[:, :, :own], 0, 1).reshape(layers, heads)
    alog = jnp.moveaxis(by_head[:, :, own : 2 * own], 0, 1).reshape(layers, heads)
    skip_ch = jnp.repeat(by_head[:, :, 2 * own : 3 * own], width // own, axis=2)
    prm = jnp.concatenate([prm[:, :, :6], skip_ch[:, :, None], prm[:, :, 7:]], axis=2)
    rate = -jnp.exp(alog)
    hp = jnp.concatenate(
        [
            jnp.tile(dtb, (1, copies))[:, None],
            jnp.tile(rate, (1, copies))[:, None],
            jnp.zeros((layers, 6, LANES), f32),
        ],
        axis=1,
    )
    cbc = jnp.concatenate(
        [conv_bc, conv_bc_bias[:, None], jnp.zeros((layers, 3, bc), f32)], axis=1
    )

    rows_b = depth // groups

    def shared_rows(i):
        both = jnp.concatenate([w_bcdt[i], in_gain[i][:, None]], axis=1)
        own_rows = lax.dynamic_slice_in_dim(both, at_t * rows_b, rows_b, 0)
        return jnp.pad(own_rows, ((0, 0), (0, width - both.shape[1])))

    def gather(pieces):
        local = jnp.concatenate(pieces, axis=0)
        got = lax.all_gather(local, ("tensor", "dp"), axis=0, tiled=False)
        return got.reshape((groups, shards) + local.shape)

    def spread_out(x, order):
        target = [pair for axis in axes for pair in reversed(bits_of(axis))]
        names = []
        for axis, bit in order:
            got = exchange(x, axis, bit)
            mine = (lax.axis_index(axis) >> bit) & 1
            dim = sum(target.index(name) < target.index((axis, bit)) for name in names)
            x = jnp.stack([jnp.where(mine == 0, x, got), jnp.where(mine == 0, got, x)], axis=dim)
            names.insert(dim, (axis, bit))
        return x.reshape((groups, shards) + x.shape[len(names) :])

    first = jnp.concatenate([w_zx[0, :, 1], shared_rows(0)], axis=0)
    half = width // 2
    ring = db[1:] + db[:1]
    first = [
        spread_out(first[:, :half], ring + tb[1:] + tb[:1]),
        spread_out(first[:, half:], ring[:-1] + tb[1:] + ring[-1:] + tb[:1]),
    ]
    head = gather(
        [w_zx[0, :, 0], w_out[0]]
        + [w_zx[i, :, 1] for i in range(1, layers)]
        + [shared_rows(i) for i in range(1, layers)]
    )
    w_x = [[(part, 0) for part in first]] + [[(head, 1 + i)] for i in range(1, layers)]
    w_z, w_o = [(head, 0)], [(head, 1)]
    for i in range(1, layers):
        later = gather([w_zx[i, :, 0], w_out[i]])
        w_z.append((later, 0))
        w_o.append((later, 1))
    wbs, gains = [], []
    for i in range(layers):
        at = (1 + layers) * depth + (i - 1) * rows_b
        held = [part[:, :, depth:] for part in first] if i == 0 else [head[:, :, at : at + rows_b]]
        got = jnp.concatenate(
            [jnp.moveaxis(part, 0, 1).reshape(model, -1)[:, : 2 * half] for part in held], axis=1
        )
        wbs.append(
            jnp.concatenate(
                [got[:, :bc], jnp.tile(got[:, bc : bc + heads], (1, copies))], axis=1
            )
        )
        gains.append(got[:, bc + heads].astype(f32))

    small = [
        ((ext, wide), f32),
        ((rows, state_n), f32),
        ((rows, state_n), f32),
        ((state_n, rows), f32),
        ((state_n, rows), f32),
        ((rows, LANES), f32),
        ((LANES, rows), f32),
        ((rows, LANES), bf16),
        ((rows, LANES), bf16),
        ((rows, LANES), bf16),
        ((rows, LANES), bf16),
        ((rows, LANES), bf16),
    ]
    prm_spec = pl.BlockSpec((1, 8, width), lambda g: (g, 0, 0))
    saved = []
    stream = hidden
    for i in range(layers):
        rinv = lax.rsqrt(jnp.mean(stream * stream, axis=-1, keepdims=True) + epsilon)
        normed = (stream * rinv * gains[i]).astype(bf16)
        before = shift(normed[rows - HALO :], "tensor", 1)
        nrm = jnp.concatenate([before, normed], axis=0)
        nrmt = jnp.concatenate(
            [normed, before, jnp.zeros((LANES - HALO, model), bf16)], axis=0
        ).T
        wb, pr = wbs[i], prm[:, i]
        flops = 2 * ext * model * (full + wide)
        outs = pl.pallas_call(
            partial(scan_in_kernel, heads, own, taps_n, len(w_x[i])),
            grid=(groups,),
            in_specs=[
                whole((ext, model)),
                *[kind_block(depth, part) for part in w_x[i]],
                whole((model, wide)),
                prm_spec,
                whole((8, bc)),
                whole((8, LANES)),
                whole((ext, 1)),
                whole((8, rows)),
            ],
            out_specs=[
                by_column(rows, width),
                by_column(ext, width),
                by_column(state_n + HALO, width),
                by_column(8, width),
            ]
            + [whole(s) for s, _ in small],
            out_shape=[
                struct(rows, full),
                struct(ext, full),
                struct(state_n + HALO, full, dtype=bf16),
                struct(8, full),
            ]
            + [struct(*s, dtype=d) for s, d in small],
            scratch_shapes=[
                pltpu.VMEM((chunks, SPAN, SPAN), f32),
                pltpu.VMEM((chunks, SPAN, SPAN), f32),
            ],
            name="scan_in",
            **params(3 * flops, 4 * rows * full * 3),
        )(nrm, *[part for part, _ in w_x[i]], wb, pr, cbc[i], hp[i], segc, segr)
        y_loc, xin, state, ftot = outs[:4]
        rest = outs[4:]
        shared, b_m, c_m, b_t, c_t, dtp, cumt, dts, es, fs, fd, cums = rest
        s_in = carry_states(state, "tensor", False)
        z, y, branch, grms, nxt = pl.pallas_call(
            partial(gate_kernel, heads, own, full),
            grid=(groups,),
            in_specs=[
                whole((ext, model)),
                kind_block(depth, w_z[i]),
                pl.BlockSpec((groups, shards, depth, width), lambda g, k=w_o[i][1]: (0, 0, k, 0)),
                by_column(rows, width),
                whole((rows, state_n)),
                whole((rows, LANES)),
                by_column(state_n, width),
                whole((groups, 8, width)),
                whole((rows, model)),
            ],
            out_specs=[
                by_column(rows, width),
                by_column(rows, width),
                whole((rows, model)),
                whole((rows, LANES)),
                whole((rows, model)),
            ],
            out_shape=[
                struct(rows, full),
                struct(rows, full),
                struct(rows, model),
                struct(rows, LANES),
                struct(rows, model),
            ],
            scratch_shapes=[
                pltpu.VMEM((rows, LANES), f32),
                pltpu.VMEM((groups, rows, width), f32),
            ],
            name="gate",
            **params(4 * rows * model * full, 4 * rows * full * 5),
        )(nrm, w_z[i][0], w_o[i][0], y_loc, c_m, fd, s_in, pr, stream)
        saved.append((stream, rinv, nrmt, xin, ftot, rest, s_in, z, y, branch, grms))
        stream = nxt

    def grad_block(count):
        return pl.BlockSpec((None, shards, count, width), lambda g: (g, 0, 0, 0))

    grad = cotangent
    x_part = None
    gain_grads, prm_grads, cbc_grads, hp_grads = [], [], [], []

    for i in reversed(range(layers)):
        stream_in, rinv, nrmt, xin, ftot, rest, s_in, z, y, branch, grms = saved[i]
        shared, b_m, c_m, b_t, c_t, dtp, cumt, dts, es, fs, fd, cums = rest
        wb, pr = wbs[i], prm[:, i]
        dbr = grad.astype(bf16)
        if x_part is not None:
            dbr, x_part, x_send = lax.optimization_barrier((dbr, x_part, x_send))
            x_got = exchange(x_send, *tb[1])
        g_zo, dy, dnz, dstate, g_gain = pl.pallas_call(
            partial(gate_back_kernel, heads, own, full),
            grid=(groups,),
            in_specs=[
                whole((rows, model)),
                whole((model, rows)),
                whole((rows, model)),
                kind_block(depth, w_o[i]),
                kind_block(depth, w_z[i]),
                by_column(rows, width),
                by_column(rows, width),
                whole((rows, LANES)),
                whole((model, rows + LANES)),
                whole((state_n, rows)),
                whole((rows, LANES)),
                prm_spec,
            ],
            out_specs=[
                grad_block(2 * depth),
                by_column(rows, width),
                whole((rows, model)),
                by_column(state_n + HALO, width),
                by_column(8, width),
            ],
            out_shape=[
                struct(groups, shards, 2 * depth, width, dtype=bf16),
                struct(rows, full),
                struct(rows, model),
                struct(state_n + HALO, full, dtype=bf16),
                struct(8, full),
            ],
            scratch_shapes=[pltpu.VMEM((rows, LANES), f32)],
            name="gate_back",
            **params(8 * rows * model * full, 4 * rows * full * 6),
        )(dbr, dbr.T, branch, w_o[i][0], w_z[i][0], z, y, grms, nrmt, c_t, fd, pr)
        if x_part is not None:
            g_zo, dy, dnz, dstate, g_gain, x_got = lax.optimization_barrier(
                (g_zo, dy, dnz, dstate, g_gain, x_got)
            )
        ds_in = carry_states(dstate, "tensor", True)
        if x_part is not None:
            x_part, _ = scatter_step(x_part, x_names, tb[1], x_got)
            later_sum = jnp.concatenate([z_part, o_part, x_part], axis=len(db))
            ds_in, later_sum = lax.optimization_barrier((ds_in, later_sum))
            later_sum = lax.psum_scatter(
                later_sum.reshape((shards,) + later_sum.shape[len(db) :]),
                "dp",
                scatter_dimension=0,
                tiled=False,
            )
        chains = []
        for part, order in (
            (g_zo[:, :, :depth], order_x),
            (g_zo[:, :, depth:], order_y if i == 0 else order_x),
        ):
            part, names = scatter_step(*scatter_start(part, axes), order[0])
            chains.append((part, names, order[1], outgoing(part, names, order[1])))
        (z_part, z_names, z_pair, z_send), (o_part, o_names, o_pair, o_send) = chains
        ds_in, z_part, o_part, z_send, o_send = lax.optimization_barrier(
            (ds_in, z_part, o_part, z_send, o_send)
        )
        z_got = exchange(z_send, *z_pair)
        o_got = exchange(o_send, *o_pair)
        g_x, g_b, dn, g_prm, g_cbc, g_hp = pl.pallas_call(
            partial(scan_back_kernel, heads, own, taps_n, len(w_x[i])),
            grid=(groups,),
            in_specs=[
                by_column(ext, width),
                by_column(rows, width),
                by_column(rows, width),
                by_column(state_n, width),
                by_column(state_n, width),
                *[kind_block(depth, part) for part in w_x[i]],
                whole((model, wide)),
                prm_spec,
                whole((8, bc)),
                whole((8, LANES)),
                whole((ext, 1)),
                whole((8, rows)),
                whole((model, rows + LANES)),
            ]
            + [whole(s) for n, (s, _) in enumerate(small) if n != 10],
            out_specs=[
                grad_block(depth),
                whole((model, wide)),
                whole((ext, model)),
                pl.BlockSpec((1, 8, width), lambda g: (g, 0, 0)),
                whole((8, bc)),
                whole((8, LANES)),
            ],
            out_shape=[
                struct(groups, shards, depth + rows_b, width, dtype=bf16),
                struct(model, wide),
                struct(ext, model),
                struct(groups, 8, width),
                struct(8, bc),
                struct(8, LANES),
            ],
            scratch_shapes=[
                pltpu.VMEM((chunks, SPAN, SPAN), f32),
                pltpu.VMEM((chunks, SPAN, SPAN), f32),
                pltpu.VMEM((chunks, SPAN, SPAN), f32),
                pltpu.VMEM((rows, state_n), f32),
                pltpu.VMEM((rows, state_n), f32),
                pltpu.VMEM((rows, LANES), f32),
                pltpu.VMEM((rows, LANES), f32),
                pltpu.VMEM((rows + LANES, width), f32),
                pltpu.VMEM((rows + LANES, bc), f32),
                pltpu.VMEM((rows, width), f32),
            ],
            name="scan_back",
            **params(8 * rows * model * full, 4 * rows * full * 6),
        )(
            xin, dy, y, s_in, ds_in, *[part for part, _ in w_x[i]], wb, pr, cbc[i], hp[i], segc, segr, nrmt,
            shared, b_m, c_m, b_t, c_t, dtp, cumt, dts, es, fs, cums,
        )
        g_x, g_b, dn, g_prm, g_cbc, g_hp, z_got, o_got = lax.optimization_barrier(
            (g_x, g_b, dn, g_prm, g_cbc, g_hp, z_got, o_got)
        )
        z_part, z_names = scatter_step(z_part, z_names, z_pair, z_got)
        o_part, o_names = scatter_step(o_part, o_names, o_pair, o_got)
        parts_b = low(jnp.pad(g_b[:, : bc + heads], ((0, 0), (0, width - bc - heads))))
        parts_b = jnp.moveaxis(parts_b.reshape(shards, groups, rows_b, width), 1, 0)
        g_x = lax.dynamic_update_slice(g_x, parts_b, (0, 0, depth, 0))
        if i > 0:
            x_part, x_names = scatter_step(*scatter_start(g_x, axes), tb[0])
            x_send = outgoing(x_part, x_names, tb[1])
        else:
            x_full, x_names = scatter_start(g_x, axes)
            x_got = exchange(outgoing(x_full, x_names, tb[0]), *tb[0])
            chains = []
            for cut, order in ((slice(None, half), order_x), (slice(half, None), order_y)):
                part, names = scatter_step(x_full[..., cut], x_names, tb[0], x_got[..., cut])
                chains.append([part, names, list(order[1:])])
            chains.append([z_part, z_names, list(order_x[2:])])
            chains.append([o_part, o_names, [p for p in order_y if p in o_names]])
            later = (dn, g_prm, g_cbc, g_hp, g_gain)
            while any(order for _, _, order in chains):
                sends = [
                    outgoing(part, names, order[0]) if order else part for part, names, order in chains
                ]
                if later is None:
                    sends = lax.optimization_barrier(sends)
                else:
                    sends, later = lax.optimization_barrier((sends, later))
                    dn, g_prm, g_cbc, g_hp, g_gain = later
                    later = None
                gots = [
                    exchange(send, *order[0]) if order else send
                    for send, (_, _, order) in zip(sends, chains)
                ]
                for chain, got in zip(chains, gots):
                    part, names, order = chain
                    if order:
                        kind = bf16 if len(order) > 1 else f32
                        chain[0], chain[1] = scatter_step(part, names, order[0], got, kind)
                        chain[2] = order[1:]
        after = shift(dn[rows:], "tensor", -1)
        dnormed = dnz + dn[:rows]
        dnormed = jnp.concatenate(
            [dnormed[: rows - HALO], dnormed[rows - HALO :] + after], axis=0
        )
        scaled_in = stream_in * rinv
        gain_grads.append(jnp.sum(dnormed * scaled_in, axis=0))
        scaled = dnormed * gains[i]
        grad = grad + rinv * (
            scaled - scaled_in * jnp.mean(scaled * scaled_in, axis=-1, keepdims=True)
        )

        g_prm = g_prm.at[:, 5].set(g_gain[0].reshape(groups, width))
        prm_grads.append(g_prm)
        cbc_grads.append(g_cbc)
        hp_grads.append(g_hp)

    def stacked(items):
        return jnp.stack(items[::-1], axis=0)

    x_done = jnp.concatenate([chains[0][0], chains[1][0]], axis=1)
    z_done, o_done = chains[2][0], chains[3][0]
    done = [jnp.concatenate([z_done, o_done, x_done], axis=0), later_sum.astype(f32)]

    g_prm = stacked(prm_grads).swapaxes(0, 1)
    g_prm = scatter_rest(*scatter_start(g_prm, ("tensor",)), tb, f32)
    rest_sum = jnp.concatenate(
        [
            stacked(gain_grads).reshape(-1),
            stacked(cbc_grads).reshape(-1),
            stacked(hp_grads).reshape(-1),
        ]
    )
    rest_sum = all_sum(rest_sum.reshape(-1, width), tb)
    rest_sum = all_sum(jnp.concatenate([g_prm.reshape(-1, width), rest_sum], axis=0), db)
    mine = rest_sum[: 8 * layers].reshape(layers, 8, width)
    flat = rest_sum[8 * layers :].reshape(-1)
    gain_all = flat[: layers * model].reshape(layers, model)
    flat = flat[layers * model :]
    cbc_all = flat[: layers * 8 * bc].reshape(layers, 8, bc)
    hp_all = flat[layers * 8 * bc :].reshape(layers, 8, LANES)
    per = model // (groups * shards)
    grad_in_gain = lax.dynamic_slice_in_dim(gain_all, (at_d * groups + at_t) * per, per, 1)
    heads_mine = lax.dynamic_slice_in_dim(hp_all, at_t * own, own, 2)
    grad_w_zx = jnp.stack(
        [jnp.stack([d[:depth], d[2 * depth : 3 * depth]], axis=1) for d in done], axis=0
    )
    grad_w_out = jnp.stack([d[depth : 2 * depth] for d in done], axis=0)
    grad_w_bcdt = jnp.stack([d[3 * depth :, : bc + heads] for d in done], axis=0)
    return (
        stream,
        grad,
        grad_in_gain,
        grad_w_zx,
        grad_w_bcdt,
        grad_w_out,
        mine[:, :taps_n],
        mine[:, taps_n],
        cbc_all[:, :taps_n],
        cbc_all[:, taps_n],
        heads_mine[:, 0],
        heads_mine[:, 1],
        mine[:, 6].reshape(layers, own, width // own).sum(axis=-1),
        mine[:, 5],
    )


def solution(mesh):
    placed = (
        P(("dp", "tensor"), None),
        P("dp", None),
        P(None, "dp"),
        P(None, "dp", None, "tensor"),
        P(None, "dp", None),
        P(None, "dp", "tensor"),
        P(None, None, "tensor"),
        P(None, "tensor"),
        P(),
        P(),
        P(None, "tensor"),
        P(None, "tensor"),
        P(None, "tensor"),
        P(None, "tensor"),
        P(("dp", "tensor"), None),
    )
    return jax.shard_map(
        body,
        mesh=mesh,
        in_specs=placed,
        out_specs=(
            P(("dp", "tensor"), None),
            P(("dp", "tensor"), None),
            P(None, ("dp", "tensor")),
            P(None, "dp", None, "tensor"),
            P(None, ("dp", "tensor"), None),
            P(None, "dp", "tensor"),
            P(None, None, "tensor"),
            P(None, "tensor"),
            P(),
            P(),
            P(None, "tensor"),
            P(None, "tensor"),
            P(None, "tensor"),
            P(None, "tensor"),
        ),
        check_vma=False,
    )
```

```python
from functools import partial

import jax
import jax.numpy as jnp
from jax import lax
from jax.experimental import pallas as pl
from jax.experimental.pallas import tpu as pltpu
from jax.sharding import PartitionSpec as P

bf16 = jnp.bfloat16
f32 = jnp.float32
epsilon = 1e-05
SPAN = 256
HALO = 16
LANES = 128
NEG = -1e30
VMEM = 56 * 1024 * 1024


def mm(a, b):
    return lax.dot_general(a, b, (((1,), (0,)), ((), ())), preferred_element_type=f32)


def mmt(a, b):
    return lax.dot_general(a, b, (((1,), (1,)), ((), ())), preferred_element_type=f32)


def mmf(a, b):
    return lax.dot_general(
        a, b, (((1,), (0,)), ((), ())), precision=lax.Precision.HIGHEST, preferred_element_type=f32
    )


def two(x):
    first = low(x)
    return first, low(x - first.astype(f32))


def mm3(a, b):
    a0, a1 = two(a)
    b0, b1 = two(b)
    return mm(a0, b0) + (mm(a0, b1) + mm(a1, b0))


def mmt3(a, b):
    a0, a1 = two(a)
    b0, b1 = two(b)
    return mmt(a0, b0) + (mmt(a0, b1) + mmt(a1, b0))


def iota(shape, axis):
    return lax.broadcasted_iota(jnp.int32, shape, axis)


def low(x):
    return x.astype(bf16)


def three(x):
    first = low(x).astype(f32)
    rest = x - first
    second = low(rest).astype(f32)
    return first, second, rest - second


def split_heads(x, heads):
    first, second, third = three(x)
    part = iota(x.shape, 1) // heads
    zero = jnp.zeros_like(x)
    return low(
        jnp.where(part == 0, first, jnp.where(part == 1, second, jnp.where(part == 2, third, zero)))
    )


def spread(group, heads, own, width):
    row, col = iota((LANES, width), 0), iota((LANES, width), 1)
    return low(
        ((row % heads == group * own + col // (width // own)) & (row < 3 * heads)).astype(f32)
    )


def pick(group, heads, own):
    row, col = iota((LANES, LANES), 0), iota((LANES, LANES), 1)
    return low(((row % heads == group * own + col) & (col < own) & (row < 3 * heads)).astype(f32))


def gather_heads(x, group, own):
    width = x.shape[1]
    row, col = iota((width, LANES), 0), iota((width, LANES), 1)
    fold = low((col == group * own + row // (width // own)).astype(f32))
    first, second, third = three(x)
    return mm(low(first), fold) + mm(low(second), fold) + mm(low(third), fold)


def keeps(segc, rows):
    now = segc[HALO : HALO + rows]
    return [None] + [
        (segc[HALO - j : HALO - j + rows] == now).astype(f32) for j in range(1, 4)
    ]


def conv(ext, taps, keep, rows, count):
    total = taps[count : count + 1] + taps[0:1] * ext[HALO : HALO + rows]
    for j in range(1, count):
        total = total + taps[j : j + 1] * (ext[HALO - j : HALO - j + rows] * keep[j])
    return total


def triangle(rows, lower):
    row, col = iota((rows, rows), 0), iota((rows, rows), 1)
    return ((row >= col) if lower else (row <= col)).astype(f32)


def scan_in_kernel(heads, own, taps_n, pieces, halo, nrm, *refs):
    w, refs = refs[:pieces], refs[pieces:]
    (
        wb,
        prm,
        cbc,
        hp,
        segc,
        segr,
        y,
        xin,
        state,
        ftot,
        shared,
        b_out,
        c_out,
        bt_out,
        ct_out,
        dtp_out,
        cumt_out,
        dts_out,
        es_out,
        fs_out,
        fd_out,
        cums_out,
        g_scr,
        m_scr,
    ) = refs
    group = pl.program_id(0)
    rows = y.shape[0]
    width = y.shape[1]
    chunks = rows // SPAN
    keep = keeps(segc[...], rows)

    @pl.when(group == 0)
    def _():
        sh = jnp.concatenate([mm(halo[...], wb[...]), mm(nrm[...], wb[...])], axis=0)
        shared[...] = sh
        half = cbc.shape[1] // 2
        act = conv(sh[:, : 2 * half], cbc[...], keep, rows, taps_n)
        act = act * jax.nn.sigmoid(act)
        bmat, cmat = act[:, :half], act[:, half:]
        b_out[...] = bmat
        c_out[...] = cmat
        bt_out[...] = bmat.T
        ct_out[...] = cmat.T
        dtp = sh[HALO:, 2 * half :] + hp[0:1]
        dtp_out[...] = dtp
        dt = jnp.maximum(dtp, 0.0) + jnp.log1p(jnp.exp(-jnp.abs(dtp)))
        cum = mmf(triangle(rows, True), dt * hp[1:2])
        cumt_out[...] = cum.T
        dts_out[...] = split_heads(dt, heads)
        cums_out[...] = split_heads(cum, heads)
        seg = segc[...]
        here = seg[HALO:]
        fd_out[...] = split_heads(
            jnp.exp(cum) * (here == seg[HALO - 1 : HALO]).astype(f32), heads
        )
        for c in range(chunks):
            lo, hi = c * SPAN, (c + 1) * SPAN
            block = cum[lo:hi]
            base = jnp.zeros_like(cum[0:1]) if c == 0 else cum[lo - 1 : lo]
            before = seg[HALO + lo - 1 : HALO + lo]
            last = here[hi - 1 : hi]
            fs_out[lo:hi] = split_heads(
                jnp.exp(block - base) * (here[lo:hi] == before).astype(f32), heads
            )
            es_out[lo:hi] = split_heads(
                jnp.exp(cum[hi - 1 : hi] - block) * (here[lo:hi] == last).astype(f32), heads
            )
            g_scr[c] = mmt3(cmat[lo:hi], bmat[lo:hi])
            ok = (here[lo:hi] == segr[0:1, lo:hi]) & (
                iota((SPAN, SPAN), 0) >= iota((SPAN, SPAN), 1)
            )
            m_scr[c] = jnp.where(ok, 0.0, NEG)

    weight = [part[...].reshape(nrm.shape[1], -1) for part in w]
    ext = jnp.concatenate(
        [
            jnp.concatenate([mm(source[...], part) for part in weight], axis=1)
            for source in (halo, nrm)
        ],
        axis=0,
    )
    xin[...] = ext
    u = conv(ext, prm[0], keep, rows, taps_n)
    xc = u * jax.nn.sigmoid(u)
    grow = spread(group, heads, own, width)
    xd = xc * mm(dts_out[...], grow)
    xd0, xd1 = two(xd)
    exd = xd * mm(es_out[...], grow)
    fx = mm(fs_out[...], grow)
    cols = mm(cums_out[...], pick(group, heads, own))
    rowsum = cumt_out[pl.ds(pl.multiple_of(group * own, own), own), :]
    per = width // own
    side = iota((SPAN, 2 * per), 1) < per
    now = None
    for c in range(chunks):
        lo, hi = c * SPAN, (c + 1) * SPAN
        m, g = m_scr[c], g_scr[c]
        for pair in range(own // 2):
            at = slice(2 * per * pair, 2 * per * (pair + 1))
            x2 = jnp.concatenate([xd0[lo:hi, at], xd1[lo:hi, at]], axis=1)
            out = []
            for h in (2 * pair, 2 * pair + 1):
                decay = jnp.exp(cols[lo:hi, h : h + 1] - rowsum[h : h + 1, lo:hi] + m)
                both = mm(low(decay * g), x2)
                out.append(both[:, : 2 * per] + both[:, 2 * per :])
            y[lo:hi, at] = (
                jnp.where(side, out[0], out[1]) + prm[0, 6:7, at] * xc[lo:hi, at]
            )
        local = mm3(bt_out[:, lo:hi], exd[lo:hi])
        if c > 0:
            y[lo:hi] += fx[lo:hi] * mm3(c_out[lo:hi], now)
            now = fx[hi - 1 : hi] * now + local
        else:
            now = local
    whole_factor = mm(fd_out[...], grow)[rows - 1 : rows]
    ftot[...] = jnp.broadcast_to(whole_factor, ftot.shape)
    put_state(state, now, whole_factor)


def gate_kernel(
    heads,
    own,
    full,
    nrm,
    wz,
    wo,
    y_loc,
    c_in,
    fd,
    s_in,
    prm,
    hid,
    z_out,
    y_out,
    branch,
    grms,
    nxt,
    ss,
    gated_scr,
):
    group = pl.program_id(0)
    width = y_loc.shape[1]
    z = mm(nrm[...], wz[...].reshape(-1, width))
    y = y_loc[...] + mm(fd[...], spread(group, heads, own, width)) * (
        lambda parts: mm(parts[0], s_in[...]) + mm(parts[1], s_in[...])
    )(two(c_in[...]))
    z_out[...] = z
    y_out[...] = y
    gated = y * (z * jax.nn.sigmoid(z))
    squares = jnp.sum(gated * gated, axis=1, keepdims=True)
    gated_scr[group] = gated

    @pl.when(group == 0)
    def _():
        ss[...] = jnp.broadcast_to(squares, ss.shape)

    @pl.when(group > 0)
    def _():
        ss[...] += jnp.broadcast_to(squares, ss.shape)

    @pl.when(group == pl.num_programs(0) - 1)
    def _():
        scale = lax.rsqrt(ss[...] / full + epsilon)
        grms[...] = scale
        total = None
        for g in range(prm.shape[0]):
            mixed = low(gated_scr[g] * scale[:, 0:1] * prm[g, 5:6])
            part = mmt(mixed, wo[g].reshape(-1, width))
            total = part if total is None else total + part
        branch[...] = total
        nxt[...] = hid[...] + total


def gate_back_kernel(
    heads,
    own,
    full,
    dbr,
    dbrt,
    branch,
    wo,
    wz,
    z_in,
    y_in,
    grms,
    nrmt,
    ct,
    fd,
    prm,
    g_zo,
    dy_out,
    dn,
    dstate,
    g_gain,
    q_scr,
):
    group = pl.program_id(0)
    rows, width = z_in.shape
    depth = wz.shape[1]
    block = wz.shape

    @pl.when(group == 0)
    def _():
        inner = jnp.sum(dbr[...].astype(f32) * branch[...], axis=1, keepdims=True)
        q_scr[...] = grms[...] * grms[...] * (inner / full)

    rms = grms[:, 0:1]
    dm = mm(dbr[...], wo[...].reshape(-1, width))
    z, y = z_in[...], y_in[...]
    sg = jax.nn.sigmoid(z)
    sz = z * sg
    gated = y * sz
    scaled = gated * rms
    gain = prm[0, 5:6]
    g_zo[:, depth:] = low(mm(dbrt[...], low(scaled * gain))).reshape(block)
    g_gain[...] = jnp.broadcast_to(jnp.sum(dm * scaled, axis=0, keepdims=True), g_gain.shape)
    dg = rms * (dm * gain) - gated * q_scr[:, 0:1]
    dy = dg * sz
    dy_out[...] = dy
    dz = low(dg * y * (sg + sz * (1.0 - sg)))
    g_zo[:, :depth] = low(mm(nrmt[:, :rows], dz)).reshape(block)
    part = mmt(dz, wz[...].reshape(-1, width))

    @pl.when(group == 0)
    def _():
        dn[...] = part

    @pl.when(group > 0)
    def _():
        dn[...] += part

    fx = mm(fd[...], spread(group, heads, own, width))
    put_state(dstate, mm3(ct[...], fx * dy), fx[rows - 1 : rows])


def put_state(state, now, factor):
    high, rest = two(factor)
    count = state.shape[0] - now.shape[0]
    row = iota((count, factor.shape[1]), 0)
    tail = jnp.where(row == 0, high.astype(f32), jnp.where(row == 1, rest.astype(f32), 0.0))
    state[...] = low(jnp.concatenate([now, tail], axis=0))


def conv_back(du, ext, taps, keep, rows, count, dest):
    dest[...] = jnp.zeros_like(dest)
    dest[0:rows] = taps[0:1] * du
    sums = [jnp.sum(du * ext[HALO : HALO + rows], axis=0, keepdims=True)]
    for j in range(1, count):
        kept = du * keep[j]
        sums.append(jnp.sum(kept * ext[HALO - j : HALO - j + rows], axis=0, keepdims=True))
        moved = taps[j : j + 1] * kept
        dest[0 : rows - j] += moved[j:]
        dest[rows + HALO - j : rows + HALO] += moved[:j]
    return sums, jnp.sum(du, axis=0, keepdims=True)


def scan_back_kernel(heads, own, taps_n, pieces, xin, dy_in, y_in, s_in, ds_in, dnz, *refs):
    w, refs = refs[:pieces], refs[pieces:]
    (
        wb,
        prm,
        cbc,
        hp,
        segc,
        segr,
        nrmt,
        shared,
        b_in,
        c_in,
        bt,
        ct,
        dtp,
        cumt,
        dts,
        es,
        fs,
        cums,
        g_x,
        g_b,
        dn,
        g_prm,
        g_cbc,
        g_hp,
        gt_scr,
        mt_scr,
        dgt_scr,
        db_scr,
        dc_scr,
        dcum_scr,
        ddt_scr,
        dx_scr,
        dbc_scr,
        dxc_scr,
    ) = refs
    group = pl.program_id(0)
    rows, width = dy_in.shape
    chunks = rows // SPAN
    keep = keeps(segc[...], rows)

    @pl.when(group == 0)
    def _():
        here = segc[HALO:]
        for c in range(chunks):
            lo, hi = c * SPAN, (c + 1) * SPAN
            gt_scr[c] = mmt3(b_in[lo:hi], c_in[lo:hi])
            ok = (here[lo:hi] == segr[0:1, lo:hi]) & (
                iota((SPAN, SPAN), 0) <= iota((SPAN, SPAN), 1)
            )
            mt_scr[c] = jnp.where(ok, 0.0, NEG)
        for ref in (dgt_scr, db_scr, dc_scr, dcum_scr, ddt_scr):
            ref[...] = jnp.zeros_like(ref)

    u = conv(xin[...], prm[0], keep, rows, taps_n)
    sg = jax.nn.sigmoid(u)
    xc = u * sg
    grow = spread(group, heads, own, width)
    dtx = mm(dts[...], grow)
    ex = mm(es[...], grow)
    fx = mm(fs[...], grow)
    xd = xc * dtx
    xd0, xd1 = two(xd)
    exd = xd * ex
    cols = mm(cums[...], pick(group, heads, own))
    rowsum = cumt[pl.ds(pl.multiple_of(group * own, own), own), :]
    dy = dy_in[...]
    dyb = low(dy)
    fdy = fx * dy
    skip = prm[0, 6:7]
    per = width // own
    side = iota((SPAN, 2 * per), 1) < per
    wide_side = (iota((SPAN, 4 * per), 1) // per) % 2 == 0
    states = [s_in[...].astype(f32)]
    for c in range(chunks - 1):
        lo, hi = c * SPAN, (c + 1) * SPAN
        states.append(fx[hi - 1 : hi] * states[-1] + mm3(bt[:, lo:hi], exd[lo:hi]))
    ds = ds_in[...].astype(f32)
    for c in reversed(range(chunks)):
        lo, hi = c * SPAN, (c + 1) * SPAN
        dxs = ex[lo:hi] * mm3(b_in[lo:hi], ds)
        db_scr[lo:hi] += mmt3(exd[lo:hi], ds)
        dc_scr[lo:hi] += mmt3(fdy[lo:hi], states[c])
        mt, gt = mt_scr[c], gt_scr[c]
        parts = []
        dgt = None
        for pair in range(own // 2):
            at = slice(2 * per * pair, 2 * per * (pair + 1))
            x2 = jnp.concatenate([xd0[lo:hi, at], xd1[lo:hi, at]], axis=1)
            dy2 = dyb[lo:hi, at]
            dy4 = jnp.concatenate([dy2, dy2], axis=1)
            out = []
            for k, h in enumerate((2 * pair, 2 * pair + 1)):
                decay = jnp.exp(rowsum[h : h + 1, lo:hi] - cols[lo:hi, h : h + 1] + mt)
                out.append(mm(low(decay * gt), dy2))
                mine = wide_side if k == 0 else jnp.logical_not(wide_side)
                dw = mmt(jnp.where(mine, x2, jnp.zeros_like(x2)), dy4) * decay
                dgt = dw if dgt is None else dgt + dw
            parts.append(jnp.where(side, out[0], out[1]))
        dgt_scr[c] += dgt
        dxd = jnp.concatenate(parts, axis=1) + dxs
        xcc = xc[lo:hi]
        xdf = xd[lo:hi]
        scanned = y_in[lo:hi] - skip * xcc
        dcum_scr[lo:hi] += gather_heads(
            dyb[lo:hi].astype(f32) * scanned - xdf * dxd, group, own
        )
        tail = jnp.sum(xdf * dxs, axis=0, keepdims=True) + fx[hi - 1 : hi] * jnp.sum(
            ds * states[c], axis=0, keepdims=True
        )
        tail8 = gather_heads(jnp.broadcast_to(tail, (8, width)), group, own)
        lastrow = (iota((8, LANES), 0) == 7).astype(f32)
        dcum_scr[hi - 8 : hi] += tail8 * lastrow
        ddt_scr[lo:hi] += gather_heads(xcc * dxd, group, own)
        dxc_scr[lo:hi] = dtx[lo:hi] * dxd + skip * dy[lo:hi]
        ds = fx[hi - 1 : hi] * ds + mm3(ct[:, lo:hi], fdy[lo:hi])
    du = dxc_scr[...] * (sg + xc * (1.0 - sg))
    sums, bias = conv_back(du, xin[...], prm[0], keep, rows, taps_n, dx_scr)
    g_skip = jnp.sum(dy * xc, axis=0, keepdims=True)
    for j in range(taps_n):
        g_prm[0, j : j + 1] = sums[j]
    g_prm[0, taps_n : taps_n + 1] = bias
    g_prm[0, 5:6] = jnp.zeros_like(bias)
    g_prm[0, 6:7] = g_skip
    g_prm[0, 7:8] = jnp.zeros_like(bias)
    dxb = low(dx_scr[...])
    g_x[...] = low(mm(nrmt[...], dxb)).reshape(g_x.shape)
    part, step = None, width // pieces
    for n, weight in enumerate(w):
        term = mmt(
            dxb[: rows + HALO, n * step : (n + 1) * step],
            weight[...].reshape(-1, step),
        )
        part = term if part is None else part + term

    @pl.when(group == 0)
    def _():
        dn[0:rows] = dnz[...] + part[:rows]
        dn[rows:] = part[rows:]

    @pl.when(group > 0)
    def _():
        dn[...] += part

    @pl.when(group == pl.num_programs(0) - 1)
    def _():
        half = cbc.shape[1] // 2
        dact = []
        for c in range(chunks):
            lo, hi = c * SPAN, (c + 1) * SPAN
            dgt = dgt_scr[c]
            db_scr[lo:hi] += mm3(dgt, c_in[lo:hi])
            dc_scr[lo:hi] += mm3(dgt.T, b_in[lo:hi])
        sh = shared[:, : 2 * half]
        ubc = conv(sh, cbc[...], keep, rows, taps_n)
        sgb = jax.nn.sigmoid(ubc)
        dact = jnp.concatenate([db_scr[...], dc_scr[...]], axis=1)
        dub = dact * (sgb + ubc * sgb * (1.0 - sgb))
        bsums, bbias = conv_back(dub, sh, cbc[...], keep, rows, taps_n, dbc_scr)
        for j in range(taps_n):
            g_cbc[j : j + 1] = bsums[j]
        g_cbc[taps_n : taps_n + 1] = bbias
        g_cbc[taps_n + 1 :] = jnp.zeros_like(g_cbc[taps_n + 1 :])
        raw = dtp[...]
        dt = jnp.maximum(raw, 0.0) + jnp.log1p(jnp.exp(-jnp.abs(raw)))
        upper = triangle(SPAN, False)
        for c in range(chunks):
            lo, hi = c * SPAN, (c + 1) * SPAN
            dcum_scr[lo:hi] = mmf(upper, dcum_scr[lo:hi])
        da = dcum_scr[...]
        rate = hp[1:2]
        first = iota((rows, LANES), 1) < heads
        ddtp = jnp.where(first, (rate * da + ddt_scr[...]) * jax.nn.sigmoid(raw), 0.0)
        g_hp[...] = jnp.zeros_like(g_hp)
        g_hp[0:1] = jnp.sum(ddtp, axis=0, keepdims=True)
        g_hp[1:2] = jnp.sum(jnp.where(first, da * dt * rate, 0.0), axis=0, keepdims=True)
        dsh = low(
            jnp.concatenate(
                [dbc_scr[...], jnp.concatenate([ddtp, jnp.zeros((LANES, LANES), f32)], axis=0)],
                axis=1,
            )
        )
        g_b[...] = jnp.zeros_like(g_b)
        g_b[:, : dsh.shape[1]] = low(mm(nrmt[...], dsh))
        dn[...] += mmt(dsh[: rows + HALO], wb[...])


def whole(shape):
    return pl.BlockSpec(shape, lambda g: (0,) * len(shape))


def by_column(rows, width):
    return pl.BlockSpec((rows, width), lambda g: (0, g))


def kind_block(depth, pair):
    weights, kind = pair
    shape = weights.shape
    return pl.BlockSpec((None, shape[1], depth, shape[3]), lambda g: (g, 0, kind, 0))


def params(flops, moved):
    return dict(
        compiler_params=pltpu.CompilerParams(vmem_limit_bytes=VMEM),
        cost_estimate=pl.CostEstimate(flops=flops, bytes_accessed=moved, transcendentals=0),
    )


def struct(*shape, dtype=f32):
    return jax.ShapeDtypeStruct(shape, dtype)


def shift(x, axis, step):
    size = lax.axis_size(axis)
    return lax.ppermute(
        x, axis, [(i, i + step) for i in range(size) if 0 <= i + step < size]
    )


def bits_of(axis):
    return [(axis, b) for b in range(lax.axis_size(axis).bit_length() - 1)]


def exchange(x, axis, bit):
    return lax.ppermute(x, axis, [(i, i ^ (1 << bit)) for i in range(lax.axis_size(axis))])


def all_sum(x, order):
    for axis, bit in order:
        x = x + exchange(x, axis, bit)
    return x


def scatter_start(x, axes):
    names = [pair for axis in axes for pair in reversed(bits_of(axis))]
    return x.reshape((2,) * len(names) + x.shape[len(axes) :]), names


def outgoing(x, names, pair):
    axis, bit = pair
    mine = (lax.axis_index(axis) >> bit) & 1
    return lax.dynamic_index_in_dim(x, 1 - mine, names.index(pair), False)


def scatter_step(x, names, pair, got=None, kind=bf16):
    axis, bit = pair
    mine = (lax.axis_index(axis) >> bit) & 1
    if got is None:
        got = exchange(outgoing(x, names, pair), axis, bit)
    x = lax.dynamic_index_in_dim(x, mine, names.index(pair), False)
    x = (x.astype(f32) + got.astype(f32)).astype(kind)
    return x, [name for name in names if name != pair]


def scatter_rest(x, names, order, kind=bf16):
    for n, pair in enumerate(order):
        x, names = scatter_step(x, names, pair, None, f32 if n + 1 == len(order) else kind)
    return x


def carry_states(packed, axis, backward, beside=lambda got: (got, None)):
    size, at = lax.axis_size(axis), lax.axis_index(axis)
    count = packed.shape[0] - HALO

    def unpack(x):
        x = x.astype(f32)
        return x[:count], x[count : count + 1] + x[count + 1 : count + 2]

    total, factor = unpack(packed)
    prefix = jnp.zeros_like(total)
    prefix_factor = jnp.ones_like(factor)
    step = 1
    while step < size:
        upper = ((at // step) % 2) == 1
        follows = jnp.logical_not(upper) if backward else upper
        pairs = [(i, i ^ step) for i in range(size)]
        final = 2 * step >= size
        if final:
            pairs = [p for p in pairs if (p[0] > p[1]) == backward]
        got = lax.ppermute(packed, axis, pairs)
        if final:
            got, beside = beside(got)
        other, other_factor = unpack(got)
        prefix = jnp.where(follows, prefix_factor * other + prefix, prefix)
        if not final:
            prefix_factor = jnp.where(follows, prefix_factor * other_factor, prefix_factor)
            total = jnp.where(follows, factor * other + total, other_factor * total + other)
            factor = factor * other_factor
            high, rest = two(factor)
            packed = jnp.concatenate(
                [low(total), high, rest, jnp.zeros((HALO - 2, factor.shape[1]), bf16)], axis=0
            )
        step *= 2
    return low(prefix), beside


def body(
    hidden,
    segment_ids,
    in_gain,
    w_zx,
    w_bcdt,
    w_out,
    conv_x,
    conv_x_bias,
    conv_bc,
    conv_bc_bias,
    dt_bias,
    a_log,
    d_skip,
    out_gain,
    cotangent,
):
    layers, taps_n = conv_x.shape[0], conv_x.shape[1]
    groups, shards = lax.axis_size("tensor"), lax.axis_size("dp")
    tb, db = bits_of("tensor"), bits_of("dp")
    axes = ("tensor", "dp")
    order_x = tb + db
    order_y = tb[:1] + db[:1] + tb[1:] + db[1:]
    at_t = lax.axis_index("tensor")
    at_d = lax.axis_index("dp")
    own = dt_bias.shape[1]
    heads = own * groups
    width = out_gain.shape[1]
    full = width * groups
    rows, model = hidden.shape
    bc = conv_bc.shape[2]
    state_n = bc // 2
    depth = w_zx.shape[1]
    ext = rows + HALO
    chunks = rows // SPAN
    wide = bc + LANES
    copies = LANES // heads

    padded = jnp.pad(segment_ids.reshape(-1), (HALO, 0), constant_values=-1)
    seg = lax.dynamic_slice_in_dim(padded, at_t * rows, ext).astype(f32)
    segc = seg[:, None]
    segr = jnp.broadcast_to(seg[None, HALO:], (8, rows))

    heads_row = jnp.pad(
        jnp.concatenate([dt_bias, a_log, d_skip], axis=1), ((0, 0), (0, width - 3 * own))
    )
    pack = jnp.concatenate(
        [
            conv_x,
            conv_x_bias[:, None],
            out_gain[:, None],
            heads_row[:, None],
            jnp.zeros((layers, 1, width), f32),
        ],
        axis=1,
    )
    prm = lax.all_gather(pack, "tensor", axis=0, tiled=False)
    by_head = prm[:, :, 6]
    dtb = jnp.moveaxis(by_head[:, :, :own], 0, 1).reshape(layers, heads)
    alog = jnp.moveaxis(by_head[:, :, own : 2 * own], 0, 1).reshape(layers, heads)
    skip_ch = jnp.repeat(by_head[:, :, 2 * own : 3 * own], width // own, axis=2)
    prm = jnp.concatenate([prm[:, :, :6], skip_ch[:, :, None], prm[:, :, 7:]], axis=2)
    rate = -jnp.exp(alog)
    hp = jnp.concatenate(
        [
            jnp.tile(dtb, (1, copies))[:, None],
            jnp.tile(rate, (1, copies))[:, None],
            jnp.zeros((layers, 6, LANES), f32),
        ],
        axis=1,
    )
    cbc = jnp.concatenate(
        [conv_bc, conv_bc_bias[:, None], jnp.zeros((layers, 3, bc), f32)], axis=1
    )

    rows_b = depth // groups

    def shared_rows(i):
        both = jnp.concatenate([w_bcdt[i], in_gain[i][:, None]], axis=1)
        own_rows = lax.dynamic_slice_in_dim(both, at_t * rows_b, rows_b, 0)
        return jnp.pad(own_rows, ((0, 0), (0, width - both.shape[1])))

    def gather(pieces, after=None):
        local = jnp.concatenate(pieces, axis=0)
        if after is not None:
            local, _ = lax.optimization_barrier((local, after))
        got = lax.all_gather(local, ("tensor", "dp"), axis=0, tiled=False)
        return got.reshape((groups, shards) + local.shape)

    def spread_out(x, order):
        target = [pair for axis in axes for pair in reversed(bits_of(axis))]
        names = []
        for axis, bit in order:
            got = exchange(x, axis, bit)
            mine = (lax.axis_index(axis) >> bit) & 1
            dim = sum(target.index(name) < target.index((axis, bit)) for name in names)
            x = jnp.stack([jnp.where(mine == 0, x, got), jnp.where(mine == 0, got, x)], axis=dim)
            names.insert(dim, (axis, bit))
        return x.reshape((groups, shards) + x.shape[len(names) :])

    first = jnp.concatenate([w_zx[0, :, 1], shared_rows(0)], axis=0)
    half = width // 2
    ring = db[1:] + db[:1]
    right = spread_out(first[:, half:], ring[:-1] + tb[1:] + ring[-1:] + tb[:1])
    first = [spread_out(first[:, :half], ring + tb[1:] + tb[:1]), right]
    head = gather(
        [w_zx[0, :, 0], w_out[0]]
        + [w_zx[i, :, 1] for i in range(1, layers)]
        + [shared_rows(i) for i in range(1, layers)],
    )
    w_x = [[(part, 0) for part in first]] + [[(head, 1 + i)] for i in range(1, layers)]
    w_z, w_o = [(head, 0)], [(head, 1)]
    for i in range(1, layers):
        later = gather([w_zx[i, :, 0], w_out[i]])
        w_z.append((later, 0))
        w_o.append((later, 1))
    wbs, gains = [], []
    for i in range(layers):
        at = (1 + layers) * depth + (i - 1) * rows_b
        held = [part[:, :, depth:] for part in first] if i == 0 else [head[:, :, at : at + rows_b]]
        got = jnp.concatenate(
            [jnp.moveaxis(part, 0, 1).reshape(model, -1)[:, : 2 * half] for part in held], axis=1
        )
        wbs.append(
            jnp.concatenate(
                [got[:, :bc], jnp.tile(got[:, bc : bc + heads], (1, copies))], axis=1
            )
        )
        gains.append(got[:, bc + heads].astype(f32))

    small = [
        ((ext, wide), f32),
        ((rows, state_n), f32),
        ((rows, state_n), f32),
        ((state_n, rows), f32),
        ((state_n, rows), f32),
        ((rows, LANES), f32),
        ((LANES, rows), f32),
        ((rows, LANES), bf16),
        ((rows, LANES), bf16),
        ((rows, LANES), bf16),
        ((rows, LANES), bf16),
        ((rows, LANES), bf16),
    ]
    prm_spec = pl.BlockSpec((1, 8, width), lambda g: (g, 0, 0))
    saved = []
    stream = hidden
    for i in range(layers):
        rinv = lax.rsqrt(jnp.mean(stream * stream, axis=-1, keepdims=True) + epsilon)
        normed = (stream * rinv * gains[i]).astype(bf16)
        before = shift(normed[rows - HALO :], "tensor", 1)
        nrmt = jnp.concatenate(
            [normed, before, jnp.zeros((LANES - HALO, model), bf16)], axis=0
        ).T
        wb, pr = wbs[i], prm[:, i]
        flops = 2 * ext * model * (full + wide)
        outs = pl.pallas_call(
            partial(scan_in_kernel, heads, own, taps_n, len(w_x[i])),
            grid=(groups,),
            in_specs=[
                whole((HALO, model)),
                whole((rows, model)),
                *[kind_block(depth, part) for part in w_x[i]],
                whole((model, wide)),
                prm_spec,
                whole((8, bc)),
                whole((8, LANES)),
                whole((ext, 1)),
                whole((8, rows)),
            ],
            out_specs=[
                by_column(rows, width),
                by_column(ext, width),
                by_column(state_n + HALO, width),
                by_column(8, width),
            ]
            + [whole(s) for s, _ in small],
            out_shape=[
                struct(rows, full),
                struct(ext, full),
                struct(state_n + HALO, full, dtype=bf16),
                struct(8, full),
            ]
            + [struct(*s, dtype=d) for s, d in small],
            scratch_shapes=[
                pltpu.VMEM((chunks, SPAN, SPAN), f32),
                pltpu.VMEM((chunks, SPAN, SPAN), f32),
            ],
            name="scan_in",
            **params(3 * flops, 4 * rows * full * 3),
        )(before, normed, *[part for part, _ in w_x[i]], wb, pr, cbc[i], hp[i], segc, segr)
        y_loc, xin, state, ftot = outs[:4]
        rest = outs[4:]
        shared, b_m, c_m, b_t, c_t, dtp, cumt, dts, es, fs, fd, cums = rest
        s_in, _ = carry_states(state, "tensor", False)
        z, y, branch, grms, nxt = pl.pallas_call(
            partial(gate_kernel, heads, own, full),
            grid=(groups,),
            in_specs=[
                whole((rows, model)),
                kind_block(depth, w_z[i]),
                pl.BlockSpec((groups, shards, depth, width), lambda g, k=w_o[i][1]: (0, 0, k, 0)),
                by_column(rows, width),
                whole((rows, state_n)),
                whole((rows, LANES)),
                by_column(state_n, width),
                whole((groups, 8, width)),
                whole((rows, model)),
            ],
            out_specs=[
                by_column(rows, width),
                by_column(rows, width),
                whole((rows, model)),
                whole((rows, LANES)),
                whole((rows, model)),
            ],
            out_shape=[
                struct(rows, full),
                struct(rows, full),
                struct(rows, model),
                struct(rows, LANES),
                struct(rows, model),
            ],
            scratch_shapes=[
                pltpu.VMEM((rows, LANES), f32),
                pltpu.VMEM((groups, rows, width), f32),
            ],
            name="gate",
            **params(4 * rows * model * full, 4 * rows * full * 5),
        )(normed, w_z[i][0], w_o[i][0], y_loc, c_m, fd, s_in, pr, stream)
        saved.append((stream, rinv, nrmt, xin, ftot, rest, s_in, z, y, branch, grms))
        stream = nxt

    def grad_block(count):
        return pl.BlockSpec((None, shards, count, width), lambda g: (g, 0, 0, 0))

    def finish(i, grad, dn, after):
        stream_in, rinv = saved[i][:2]
        dnormed = jnp.concatenate(
            [dn[: rows - HALO], dn[rows - HALO : rows] + after], axis=0
        )
        scaled_in = stream_in * rinv
        gain_grads.append(jnp.sum(dnormed * scaled_in, axis=0))
        scaled = dnormed * gains[i]
        return grad + rinv * (
            scaled - scaled_in * jnp.mean(scaled * scaled_in, axis=-1, keepdims=True)
        )

    def keep_small(g_gain, g_prm, g_cbc, g_hp):
        prm_grads.append(g_prm.at[:, 5].set(g_gain[0].reshape(groups, width)))
        cbc_grads.append(g_cbc)
        hp_grads.append(g_hp)

    def stacked(items):
        return jnp.stack(items[::-1], axis=0)

    grad = cotangent
    x_part = None
    gain_grads, prm_grads, cbc_grads, hp_grads = [], [], [], []

    for i in reversed(range(layers)):
        stream_in, rinv, nrmt, xin, ftot, rest, s_in, z, y, branch, grms = saved[i]
        shared, b_m, c_m, b_t, c_t, dtp, cumt, dts, es, fs, fd, cums = rest
        wb, pr = wbs[i], prm[:, i]
        dbr = grad.astype(bf16)
        if x_part is not None:
            dbr, x_part, x_send = lax.optimization_barrier((dbr, x_part, x_send))
            x_got = exchange(x_send, *tb[1])
        g_zo, dy, dnz, dstate, g_gain = pl.pallas_call(
            partial(gate_back_kernel, heads, own, full),
            grid=(groups,),
            in_specs=[
                whole((rows, model)),
                whole((model, rows)),
                whole((rows, model)),
                kind_block(depth, w_o[i]),
                kind_block(depth, w_z[i]),
                by_column(rows, width),
                by_column(rows, width),
                whole((rows, LANES)),
                whole((model, rows + LANES)),
                whole((state_n, rows)),
                whole((rows, LANES)),
                prm_spec,
            ],
            out_specs=[
                grad_block(2 * depth),
                by_column(rows, width),
                whole((rows, model)),
                by_column(state_n + HALO, width),
                by_column(8, width),
            ],
            out_shape=[
                struct(groups, shards, 2 * depth, width, dtype=bf16),
                struct(rows, full),
                struct(rows, model),
                struct(state_n + HALO, full, dtype=bf16),
                struct(8, full),
            ],
            scratch_shapes=[pltpu.VMEM((rows, LANES), f32)],
            name="gate_back",
            **params(8 * rows * model * full, 4 * rows * full * 6),
        )(dbr, dbr.T, branch, w_o[i][0], w_z[i][0], z, y, grms, nrmt, c_t, fd, pr)
        if x_part is not None:
            g_zo, dy, dnz, dstate, g_gain, x_got = lax.optimization_barrier(
                (g_zo, dy, dnz, dstate, g_gain, x_got)
            )
        chains = []
        for part, order in (
            (g_zo[:, :, :depth], order_x),
            (g_zo[:, :, depth:], order_y if i == 0 else order_x),
        ):
            part, names = scatter_step(*scatter_start(part, axes), order[0])
            chains.append((part, names, order[1], outgoing(part, names, order[1])))
        (z_new, z_names, z_pair, z_send), (o_new, o_names, o_pair, o_send) = chains
        held = [z_new, o_new, z_send, o_send]
        if x_part is not None:
            x_part, _ = scatter_step(x_part, x_names, tb[1], x_got)
            held.append(jnp.concatenate([z_part, o_part, x_part], axis=len(db)))
        ds_in, held = carry_states(
            dstate, "tensor", True, lambda got: lax.optimization_barrier((got, held))
        )
        z_part, o_part, z_send, o_send = held[:4]
        if x_part is not None:
            later_sum = lax.psum_scatter(
                held[4].reshape((shards,) + held[4].shape[len(db) :]),
                "dp",
                scatter_dimension=0,
                tiled=False,
            )
        z_got = exchange(z_send, *z_pair)
        o_got = exchange(o_send, *o_pair)
        g_x, g_b, dn, g_prm, g_cbc, g_hp = pl.pallas_call(
            partial(scan_back_kernel, heads, own, taps_n, len(w_x[i])),
            grid=(groups,),
            in_specs=[
                by_column(ext, width),
                by_column(rows, width),
                by_column(rows, width),
                by_column(state_n, width),
                by_column(state_n, width),
                whole((rows, model)),
                *[kind_block(depth, part) for part in w_x[i]],
                whole((model, wide)),
                prm_spec,
                whole((8, bc)),
                whole((8, LANES)),
                whole((ext, 1)),
                whole((8, rows)),
                whole((model, rows + LANES)),
            ]
            + [whole(s) for n, (s, _) in enumerate(small) if n != 10],
            out_specs=[
                grad_block(depth),
                whole((model, width)),
                whole((ext, model)),
                pl.BlockSpec((1, 8, width), lambda g: (g, 0, 0)),
                whole((8, bc)),
                whole((8, LANES)),
            ],
            out_shape=[
                struct(groups, shards, depth + rows_b, width, dtype=bf16),
                struct(model, width, dtype=bf16),
                struct(ext, model),
                struct(groups, 8, width),
                struct(8, bc),
                struct(8, LANES),
            ],
            scratch_shapes=[
                pltpu.VMEM((chunks, SPAN, SPAN), f32),
                pltpu.VMEM((chunks, SPAN, SPAN), f32),
                pltpu.VMEM((chunks, SPAN, SPAN), f32),
                pltpu.VMEM((rows, state_n), f32),
                pltpu.VMEM((rows, state_n), f32),
                pltpu.VMEM((rows, LANES), f32),
                pltpu.VMEM((rows, LANES), f32),
                pltpu.VMEM((rows + LANES, width), f32),
                pltpu.VMEM((rows + LANES, bc), f32),
                pltpu.VMEM((rows, width), f32),
            ],
            name="scan_back",
            **params(8 * rows * model * full, 4 * rows * full * 6),
        )(
            xin, dy, y, s_in, ds_in, dnz, *[part for part, _ in w_x[i]], wb, pr, cbc[i], hp[i], segc, segr, nrmt,
            shared, b_m, c_m, b_t, c_t, dtp, cumt, dts, es, fs, cums,
        )
        g_x, g_b, dn, g_prm, g_cbc, g_hp, z_got, o_got = lax.optimization_barrier(
            (g_x, g_b, dn, g_prm, g_cbc, g_hp, z_got, o_got)
        )
        z_part, z_names = scatter_step(z_part, z_names, z_pair, z_got)
        o_part, o_names = scatter_step(o_part, o_names, o_pair, o_got)
        parts_b = jnp.moveaxis(g_b.reshape(shards, groups, rows_b, width), 1, 0)
        g_x = lax.dynamic_update_slice(g_x, parts_b, (0, 0, depth, 0))
        if i > 0:
            x_part, x_names = scatter_step(*scatter_start(g_x, axes), tb[0])
            x_send = outgoing(x_part, x_names, tb[1])
        else:
            break
        after = shift(dn[rows:], "tensor", -1)
        grad = finish(i, grad, dn, after)
        keep_small(g_gain, g_prm, g_cbc, g_hp)

    def together(sends, pairs, beside=()):
        sends = lax.optimization_barrier(sends)
        gots = []
        for send, pair in zip(sends, pairs):
            if pair is None:
                gots.append(shift(send, "tensor", -1))
            elif len(pair) == 3:
                size = lax.axis_size(pair[0])
                gots.append(lax.ppermute(send, pair[0], [(k, k ^ pair[1]) for k in range(size)]))
            else:
                gots.append(exchange(send, *pair))
        return lax.optimization_barrier([*gots, *beside])

    keep_small(g_gain, g_prm, g_cbc, g_hp)
    x_full, x_names = scatter_start(g_x, axes)
    x_got, after = together([outgoing(x_full, x_names, tb[0]), dn[rows:]], [tb[0], None])
    x_part, x_names = scatter_step(x_full, x_names, tb[0], x_got)
    chains = [
        [x_part[..., :half], x_names, list(order_x[1:])],
        [x_part[..., half:], x_names, list(order_y[1:])],
    ]
    chains.append([z_part, z_names, list(order_x[2:])])
    chains.append([o_part, o_names, [p for p in order_y if p in o_names]])
    grad = finish(0, grad, dn, after)
    rest_sum = jnp.concatenate(
        [
            stacked(gain_grads).reshape(-1),
            stacked(cbc_grads).reshape(-1),
            stacked(hp_grads).reshape(-1),
        ]
    ).reshape(-1, width)
    small, small_names = scatter_start(stacked(prm_grads).swapaxes(0, 1), ("tensor",))
    rounds = [[bit] for bit in tb + db[:-2]] + [db[-2:]]
    while rounds or any(order for _, _, order in chains):
        live = [chain for chain in chains if chain[2]]
        bits = rounds.pop(0) if rounds else []
        sends = [outgoing(part, names, order[0]) for part, names, order in live]
        pairs = [order[0] for _, _, order in live]
        beside = []
        if bits and bits[0] in tb:
            if bits[0] == tb[0]:
                beside = [later_sum]
            leaving = outgoing(small, small_names, bits[0])
            sends.append(jnp.concatenate([leaving.reshape(-1, width), rest_sum], axis=0))
            pairs.append(bits[0])
        elif bits:
            if small is not None:
                rest_sum = jnp.concatenate([small.reshape(-1, width), rest_sum], axis=0)
                small = None
            steps = [0]
            for _, bit in bits:
                steps += [step | (1 << bit) for step in steps]
            for step in steps[1:]:
                sends.append(rest_sum)
                pairs.append((bits[0][0], step, None))
        gots = together(sends, pairs, beside)
        if beside:
            *gots, later_sum = gots
        for chain, got in zip(live, gots):
            part, names, order = chain
            kind = f32 if len(order) == 1 else bf16
            chain[0], chain[1] = scatter_step(part, names, order[0], got, kind)
            chain[2] = order[1:]
        gots = gots[len(live) :]
        if bits and bits[0] in tb:
            count = gots[0].shape[0] - rest_sum.shape[0]
            kept_shape = outgoing(small, small_names, bits[0]).shape
            arrived = gots[0][:count].reshape(kept_shape)
            small, small_names = scatter_step(small, small_names, bits[0], arrived, f32)
            rest_sum = rest_sum + gots[0][count:]
        else:
            for got in gots:
                rest_sum = rest_sum + got
    x_done = jnp.concatenate([chains[0][0], chains[1][0]], axis=1)
    z_done, o_done = chains[2][0], chains[3][0]
    done = [jnp.concatenate([z_done, o_done, x_done], axis=0), later_sum.astype(f32)]
    mine = rest_sum[: 8 * layers].reshape(layers, 8, width)
    flat = rest_sum[8 * layers :].reshape(-1)
    gain_all = flat[: layers * model].reshape(layers, model)
    flat = flat[layers * model :]
    cbc_all = flat[: layers * 8 * bc].reshape(layers, 8, bc)
    hp_all = flat[layers * 8 * bc :].reshape(layers, 8, LANES)
    per = model // (groups * shards)
    grad_in_gain = lax.dynamic_slice_in_dim(gain_all, (at_d * groups + at_t) * per, per, 1)
    heads_mine = lax.dynamic_slice_in_dim(hp_all, at_t * own, own, 2)
    grad_w_zx = jnp.stack(
        [jnp.stack([d[:depth], d[2 * depth : 3 * depth]], axis=1) for d in done], axis=0
    )
    grad_w_out = jnp.stack([d[depth : 2 * depth] for d in done], axis=0)
    grad_w_bcdt = jnp.stack([d[3 * depth :, : bc + heads] for d in done], axis=0)
    return (
        stream,
        grad,
        grad_in_gain,
        grad_w_zx,
        grad_w_bcdt,
        grad_w_out,
        mine[:, :taps_n],
        mine[:, taps_n],
        cbc_all[:, :taps_n],
        cbc_all[:, taps_n],
        heads_mine[:, 0],
        heads_mine[:, 1],
        mine[:, 6].reshape(layers, own, width // own).sum(axis=-1),
        mine[:, 5],
    )


def solution(mesh):
    placed = (
        P(("dp", "tensor"), None),
        P("dp", None),
        P(None, "dp"),
        P(None, "dp", None, "tensor"),
        P(None, "dp", None),
        P(None, "dp", "tensor"),
        P(None, None, "tensor"),
        P(None, "tensor"),
        P(),
        P(),
        P(None, "tensor"),
        P(None, "tensor"),
        P(None, "tensor"),
        P(None, "tensor"),
        P(("dp", "tensor"), None),
    )
    return jax.shard_map(
        body,
        mesh=mesh,
        in_specs=placed,
        out_specs=(
            P(("dp", "tensor"), None),
            P(("dp", "tensor"), None),
            P(None, ("dp", "tensor")),
            P(None, "dp", None, "tensor"),
            P(None, ("dp", "tensor"), None),
            P(None, "dp", "tensor"),
            P(None, None, "tensor"),
            P(None, "tensor"),
            P(),
            P(),
            P(None, "tensor"),
            P(None, "tensor"),
            P(None, "tensor"),
            P(None, "tensor"),
        ),
        check_vma=False,
    )
```

```python
from functools import partial

import jax
import jax.numpy as jnp
from jax import lax
from jax.experimental import pallas as pl
from jax.experimental.pallas import tpu as pltpu
from jax.sharding import PartitionSpec as P

bf16 = jnp.bfloat16
f32 = jnp.float32
epsilon = 1e-05
SPAN = 256
HALO = 16
LANES = 128
NEG = -1e30
VMEM = 56 * 1024 * 1024


def mm(a, b):
    return lax.dot_general(a, b, (((1,), (0,)), ((), ())), preferred_element_type=f32)


def mmt(a, b):
    return lax.dot_general(a, b, (((1,), (1,)), ((), ())), preferred_element_type=f32)


def mmf(a, b):
    return lax.dot_general(
        a, b, (((1,), (0,)), ((), ())), precision=lax.Precision.HIGHEST, preferred_element_type=f32
    )


def two(x):
    first = low(x)
    return first, low(x - first.astype(f32))


def mm3(a, b):
    a0, a1 = two(a)
    b0, b1 = two(b)
    return mm(a0, b0) + (mm(a0, b1) + mm(a1, b0))


def mmt3(a, b):
    a0, a1 = two(a)
    b0, b1 = two(b)
    return mmt(a0, b0) + (mmt(a0, b1) + mmt(a1, b0))


def iota(shape, axis):
    return lax.broadcasted_iota(jnp.int32, shape, axis)


def low(x):
    return x.astype(bf16)


def three(x):
    first = low(x).astype(f32)
    rest = x - first
    second = low(rest).astype(f32)
    return first, second, rest - second


def split_heads(x, heads):
    first, second, third = three(x)
    part = iota(x.shape, 1) // heads
    zero = jnp.zeros_like(x)
    return low(
        jnp.where(part == 0, first, jnp.where(part == 1, second, jnp.where(part == 2, third, zero)))
    )


def spread(group, heads, own, width):
    row, col = iota((LANES, width), 0), iota((LANES, width), 1)
    return low(
        ((row % heads == group * own + col // (width // own)) & (row < 3 * heads)).astype(f32)
    )


def pick(group, heads, own):
    row, col = iota((LANES, LANES), 0), iota((LANES, LANES), 1)
    return low(((row % heads == group * own + col) & (col < own) & (row < 3 * heads)).astype(f32))


def gather_heads(x, group, own):
    width = x.shape[1]
    row, col = iota((width, LANES), 0), iota((width, LANES), 1)
    fold = low((col == group * own + row // (width // own)).astype(f32))
    first, second, third = three(x)
    return mm(low(first), fold) + mm(low(second), fold) + mm(low(third), fold)


def keeps(segc, rows):
    now = segc[HALO : HALO + rows]
    return [None] + [
        (segc[HALO - j : HALO - j + rows] == now).astype(f32) for j in range(1, 4)
    ]


def conv(ext, taps, keep, rows, count):
    total = taps[count : count + 1] + taps[0:1] * ext[HALO : HALO + rows]
    for j in range(1, count):
        total = total + taps[j : j + 1] * (ext[HALO - j : HALO - j + rows] * keep[j])
    return total


def triangle(rows, lower):
    row, col = iota((rows, rows), 0), iota((rows, rows), 1)
    return ((row >= col) if lower else (row <= col)).astype(f32)


def scan_in_kernel(heads, own, taps_n, pieces, halo, nrm, *refs):
    w, refs = refs[:pieces], refs[pieces:]
    (
        wb,
        prm,
        cbc,
        hp,
        segc,
        segr,
        y,
        xin,
        state,
        ftot,
        shared,
        b_out,
        c_out,
        bt_out,
        ct_out,
        dtp_out,
        cumt_out,
        dts_out,
        es_out,
        fs_out,
        fd_out,
        cums_out,
        g_scr,
        m_scr,
    ) = refs
    group = pl.program_id(0)
    rows = y.shape[0]
    width = y.shape[1]
    chunks = rows // SPAN
    keep = keeps(segc[...], rows)

    @pl.when(group == 0)
    def _():
        sh = jnp.concatenate([mm(halo[...], wb[...]), mm(nrm[...], wb[...])], axis=0)
        shared[...] = sh
        half = cbc.shape[1] // 2
        act = conv(sh[:, : 2 * half], cbc[...], keep, rows, taps_n)
        act = act * jax.nn.sigmoid(act)
        bmat, cmat = act[:, :half], act[:, half:]
        b_out[...] = bmat
        c_out[...] = cmat
        bt_out[...] = bmat.T
        ct_out[...] = cmat.T
        dtp = sh[HALO:, 2 * half :] + hp[0:1]
        dtp_out[...] = dtp
        dt = jnp.maximum(dtp, 0.0) + jnp.log1p(jnp.exp(-jnp.abs(dtp)))
        cum = mmf(triangle(rows, True), dt * hp[1:2])
        cumt_out[...] = cum.T
        dts_out[...] = split_heads(dt, heads)
        cums_out[...] = split_heads(cum, heads)
        seg = segc[...]
        here = seg[HALO:]
        fd_out[...] = split_heads(
            jnp.exp(cum) * (here == seg[HALO - 1 : HALO]).astype(f32), heads
        )
        for c in range(chunks):
            lo, hi = c * SPAN, (c + 1) * SPAN
            block = cum[lo:hi]
            base = jnp.zeros_like(cum[0:1]) if c == 0 else cum[lo - 1 : lo]
            before = seg[HALO + lo - 1 : HALO + lo]
            last = here[hi - 1 : hi]
            fs_out[lo:hi] = split_heads(
                jnp.exp(block - base) * (here[lo:hi] == before).astype(f32), heads
            )
            es_out[lo:hi] = split_heads(
                jnp.exp(cum[hi - 1 : hi] - block) * (here[lo:hi] == last).astype(f32), heads
            )
            g_scr[c] = mmt3(cmat[lo:hi], bmat[lo:hi])
            ok = (here[lo:hi] == segr[0:1, lo:hi]) & (
                iota((SPAN, SPAN), 0) >= iota((SPAN, SPAN), 1)
            )
            m_scr[c] = jnp.where(ok, 0.0, NEG)

    weight = [part[...].reshape(nrm.shape[1], -1) for part in w]
    ext = jnp.concatenate(
        [
            jnp.concatenate([mm(source[...], part) for part in weight], axis=1)
            for source in (halo, nrm)
        ],
        axis=0,
    )
    xin[...] = ext
    u = conv(ext, prm[0], keep, rows, taps_n)
    xc = u * jax.nn.sigmoid(u)
    grow = spread(group, heads, own, width)
    xd = xc * mm(dts_out[...], grow)
    xd0, xd1 = two(xd)
    exd = xd * mm(es_out[...], grow)
    fx = mm(fs_out[...], grow)
    cols = mm(cums_out[...], pick(group, heads, own))
    rowsum = cumt_out[pl.ds(pl.multiple_of(group * own, own), own), :]
    per = width // own
    side = iota((SPAN, 2 * per), 1) < per
    now = None
    for c in range(chunks):
        lo, hi = c * SPAN, (c + 1) * SPAN
        m, g = m_scr[c], g_scr[c]
        for pair in range(own // 2):
            at = slice(2 * per * pair, 2 * per * (pair + 1))
            x2 = jnp.concatenate([xd0[lo:hi, at], xd1[lo:hi, at]], axis=1)
            out = []
            for h in (2 * pair, 2 * pair + 1):
                decay = jnp.exp(cols[lo:hi, h : h + 1] - rowsum[h : h + 1, lo:hi] + m)
                both = mm(low(decay * g), x2)
                out.append(both[:, : 2 * per] + both[:, 2 * per :])
            y[lo:hi, at] = (
                jnp.where(side, out[0], out[1]) + prm[0, 6:7, at] * xc[lo:hi, at]
            )
        local = mm3(bt_out[:, lo:hi], exd[lo:hi])
        if c > 0:
            y[lo:hi] += fx[lo:hi] * mm3(c_out[lo:hi], now)
            now = fx[hi - 1 : hi] * now + local
        else:
            now = local
    whole_factor = mm(fd_out[...], grow)[rows - 1 : rows]
    ftot[...] = jnp.broadcast_to(whole_factor, ftot.shape)
    put_state(state, now, whole_factor)


def gate_kernel(
    heads,
    own,
    full,
    nrm,
    wz,
    wo,
    y_loc,
    c_in,
    fd,
    s_in,
    prm,
    hid,
    z_out,
    y_out,
    branch,
    grms,
    nxt,
    ss,
    gated_scr,
):
    group = pl.program_id(0)
    width = y_loc.shape[1]
    z = mm(nrm[...], wz[...].reshape(-1, width))
    y = y_loc[...] + mm(fd[...], spread(group, heads, own, width)) * (
        lambda parts: mm(parts[0], s_in[...]) + mm(parts[1], s_in[...])
    )(two(c_in[...]))
    z_out[...] = z
    y_out[...] = y
    gated = y * (z * jax.nn.sigmoid(z))
    squares = jnp.sum(gated * gated, axis=1, keepdims=True)
    gated_scr[group] = gated

    @pl.when(group == 0)
    def _():
        ss[...] = jnp.broadcast_to(squares, ss.shape)

    @pl.when(group > 0)
    def _():
        ss[...] += jnp.broadcast_to(squares, ss.shape)

    @pl.when(group == pl.num_programs(0) - 1)
    def _():
        scale = lax.rsqrt(ss[...] / full + epsilon)
        grms[...] = scale
        total = None
        for g in range(prm.shape[0]):
            mixed = low(gated_scr[g] * scale[:, 0:1] * prm[g, 5:6])
            part = mmt(mixed, wo[g].reshape(-1, width))
            total = part if total is None else total + part
        branch[...] = total
        nxt[...] = hid[...] + total


def gate_back_kernel(
    heads,
    own,
    full,
    dbr,
    dbrt,
    branch,
    wo,
    wz,
    z_in,
    y_in,
    grms,
    nrmt,
    ct,
    fd,
    prm,
    g_zo,
    dy_out,
    dn,
    dstate,
    g_gain,
    q_scr,
):
    group = pl.program_id(0)
    rows, width = z_in.shape
    depth = wz.shape[1]
    block = wz.shape

    @pl.when(group == 0)
    def _():
        inner = jnp.sum(dbr[...].astype(f32) * branch[...], axis=1, keepdims=True)
        q_scr[...] = grms[...] * grms[...] * (inner / full)

    rms = grms[:, 0:1]
    dm = mm(dbr[...], wo[...].reshape(-1, width))
    z, y = z_in[...], y_in[...]
    sg = jax.nn.sigmoid(z)
    sz = z * sg
    gated = y * sz
    scaled = gated * rms
    gain = prm[0, 5:6]
    g_zo[:, depth:] = low(mm(dbrt[...], low(scaled * gain))).reshape(block)
    g_gain[...] = jnp.broadcast_to(jnp.sum(dm * scaled, axis=0, keepdims=True), g_gain.shape)
    dg = rms * (dm * gain) - gated * q_scr[:, 0:1]
    dy = dg * sz
    dy_out[...] = dy
    dz = low(dg * y * (sg + sz * (1.0 - sg)))
    g_zo[:, :depth] = low(mm(nrmt[:, :rows], dz)).reshape(block)
    part = mmt(dz, wz[...].reshape(-1, width))

    @pl.when(group == 0)
    def _():
        dn[...] = part

    @pl.when(group > 0)
    def _():
        dn[...] += part

    fx = mm(fd[...], spread(group, heads, own, width))
    put_state(dstate, mm3(ct[...], fx * dy), fx[rows - 1 : rows])


def put_state(state, now, factor):
    high, rest = two(factor)
    count = state.shape[0] - now.shape[0]
    row = iota((count, factor.shape[1]), 0)
    tail = jnp.where(row == 0, high.astype(f32), jnp.where(row == 1, rest.astype(f32), 0.0))
    state[...] = low(jnp.concatenate([now, tail], axis=0))


def conv_back(du, ext, taps, keep, rows, count, dest):
    dest[...] = jnp.zeros_like(dest)
    dest[0:rows] = taps[0:1] * du
    sums = [jnp.sum(du * ext[HALO : HALO + rows], axis=0, keepdims=True)]
    for j in range(1, count):
        kept = du * keep[j]
        sums.append(jnp.sum(kept * ext[HALO - j : HALO - j + rows], axis=0, keepdims=True))
        moved = taps[j : j + 1] * kept
        dest[0 : rows - j] += moved[j:]
        dest[rows + HALO - j : rows + HALO] += moved[:j]
    return sums, jnp.sum(du, axis=0, keepdims=True)


def scan_back_kernel(heads, own, taps_n, pieces, xin, dy_in, y_in, s_in, ds_in, dnz, *refs):
    w, refs = refs[:pieces], refs[pieces:]
    (
        wb,
        prm,
        cbc,
        hp,
        segc,
        segr,
        nrmt,
        shared,
        b_in,
        c_in,
        bt,
        ct,
        dtp,
        cumt,
        dts,
        es,
        fs,
        cums,
        g_x,
        g_b,
        dn,
        g_prm,
        g_cbc,
        g_hp,
        gt_scr,
        mt_scr,
        dgt_scr,
        db_scr,
        dc_scr,
        dcum_scr,
        ddt_scr,
        dx_scr,
        dbc_scr,
        dxc_scr,
    ) = refs
    group = pl.program_id(0)
    rows, width = dy_in.shape
    chunks = rows // SPAN
    keep = keeps(segc[...], rows)

    @pl.when(group == 0)
    def _():
        here = segc[HALO:]
        for c in range(chunks):
            lo, hi = c * SPAN, (c + 1) * SPAN
            gt_scr[c] = mmt3(b_in[lo:hi], c_in[lo:hi])
            ok = (here[lo:hi] == segr[0:1, lo:hi]) & (
                iota((SPAN, SPAN), 0) <= iota((SPAN, SPAN), 1)
            )
            mt_scr[c] = jnp.where(ok, 0.0, NEG)
        for ref in (dgt_scr, db_scr, dc_scr, dcum_scr, ddt_scr):
            ref[...] = jnp.zeros_like(ref)

    u = conv(xin[...], prm[0], keep, rows, taps_n)
    sg = jax.nn.sigmoid(u)
    xc = u * sg
    grow = spread(group, heads, own, width)
    dtx = mm(dts[...], grow)
    ex = mm(es[...], grow)
    fx = mm(fs[...], grow)
    xd = xc * dtx
    xd0, xd1 = two(xd)
    exd = xd * ex
    cols = mm(cums[...], pick(group, heads, own))
    rowsum = cumt[pl.ds(pl.multiple_of(group * own, own), own), :]
    dy = dy_in[...]
    dyb = low(dy)
    fdy = fx * dy
    skip = prm[0, 6:7]
    per = width // own
    side = iota((SPAN, 2 * per), 1) < per
    wide_side = (iota((SPAN, 4 * per), 1) // per) % 2 == 0
    states = [s_in[...].astype(f32)]
    for c in range(chunks - 1):
        lo, hi = c * SPAN, (c + 1) * SPAN
        states.append(fx[hi - 1 : hi] * states[-1] + mm3(bt[:, lo:hi], exd[lo:hi]))
    ds = ds_in[...].astype(f32)
    for c in reversed(range(chunks)):
        lo, hi = c * SPAN, (c + 1) * SPAN
        dsb, fdyb = low(ds), low(fdy[lo:hi])
        dxs = ex[lo:hi] * mm(low(b_in[lo:hi]), dsb)
        db_scr[lo:hi] += mmt(low(exd[lo:hi]), dsb)
        dc_scr[lo:hi] += mmt(fdyb, low(states[c]))
        mt, gt = mt_scr[c], gt_scr[c]
        parts = []
        dgt = None
        for pair in range(own // 2):
            at = slice(2 * per * pair, 2 * per * (pair + 1))
            x2 = jnp.concatenate([xd0[lo:hi, at], xd1[lo:hi, at]], axis=1)
            dy2 = dyb[lo:hi, at]
            dy4 = jnp.concatenate([dy2, dy2], axis=1)
            out = []
            for k, h in enumerate((2 * pair, 2 * pair + 1)):
                decay = jnp.exp(rowsum[h : h + 1, lo:hi] - cols[lo:hi, h : h + 1] + mt)
                out.append(mm(low(decay * gt), dy2))
                mine = wide_side if k == 0 else jnp.logical_not(wide_side)
                dw = mmt(jnp.where(mine, x2, jnp.zeros_like(x2)), dy4) * decay
                dgt = dw if dgt is None else dgt + dw
            parts.append(jnp.where(side, out[0], out[1]))
        dgt_scr[c] += dgt
        dxd = jnp.concatenate(parts, axis=1) + dxs
        xcc = xc[lo:hi]
        xdf = xd[lo:hi]
        scanned = y_in[lo:hi] - skip * xcc
        dcum_scr[lo:hi] += gather_heads(
            dyb[lo:hi].astype(f32) * scanned - xdf * dxd, group, own
        )
        tail = jnp.sum(xdf * dxs, axis=0, keepdims=True) + fx[hi - 1 : hi] * jnp.sum(
            ds * states[c], axis=0, keepdims=True
        )
        tail8 = gather_heads(jnp.broadcast_to(tail, (8, width)), group, own)
        lastrow = (iota((8, LANES), 0) == 7).astype(f32)
        dcum_scr[hi - 8 : hi] += tail8 * lastrow
        ddt_scr[lo:hi] += gather_heads(xcc * dxd, group, own)
        dxc_scr[lo:hi] = dtx[lo:hi] * dxd + skip * dy[lo:hi]
        ds = fx[hi - 1 : hi] * ds + mm(low(ct[:, lo:hi]), fdyb)
    du = dxc_scr[...] * (sg + xc * (1.0 - sg))
    sums, bias = conv_back(du, xin[...], prm[0], keep, rows, taps_n, dx_scr)
    g_skip = jnp.sum(dy * xc, axis=0, keepdims=True)
    for j in range(taps_n):
        g_prm[0, j : j + 1] = sums[j]
    g_prm[0, taps_n : taps_n + 1] = bias
    g_prm[0, 5:6] = jnp.zeros_like(bias)
    g_prm[0, 6:7] = g_skip
    g_prm[0, 7:8] = jnp.zeros_like(bias)
    dxb = low(dx_scr[...])
    g_x[...] = low(mm(nrmt[...], dxb)).reshape(g_x.shape)
    part, step = None, width // pieces
    for n, weight in enumerate(w):
        term = mmt(
            dxb[: rows + HALO, n * step : (n + 1) * step],
            weight[...].reshape(-1, step),
        )
        part = term if part is None else part + term

    @pl.when(group == 0)
    def _():
        dn[0:rows] = dnz[...] + part[:rows]
        dn[rows:] = part[rows:]

    @pl.when(group > 0)
    def _():
        dn[...] += part

    @pl.when(group == pl.num_programs(0) - 1)
    def _():
        half = cbc.shape[1] // 2
        dact = []
        for c in range(chunks):
            lo, hi = c * SPAN, (c + 1) * SPAN
            dgt = dgt_scr[c]
            db_scr[lo:hi] += mm3(dgt, c_in[lo:hi])
            dc_scr[lo:hi] += mm3(dgt.T, b_in[lo:hi])
        sh = shared[:, : 2 * half]
        ubc = conv(sh, cbc[...], keep, rows, taps_n)
        sgb = jax.nn.sigmoid(ubc)
        dact = jnp.concatenate([db_scr[...], dc_scr[...]], axis=1)
        dub = dact * (sgb + ubc * sgb * (1.0 - sgb))
        bsums, bbias = conv_back(dub, sh, cbc[...], keep, rows, taps_n, dbc_scr)
        for j in range(taps_n):
            g_cbc[j : j + 1] = bsums[j]
        g_cbc[taps_n : taps_n + 1] = bbias
        g_cbc[taps_n + 1 :] = jnp.zeros_like(g_cbc[taps_n + 1 :])
        raw = dtp[...]
        dt = jnp.maximum(raw, 0.0) + jnp.log1p(jnp.exp(-jnp.abs(raw)))
        upper = triangle(SPAN, False)
        for c in range(chunks):
            lo, hi = c * SPAN, (c + 1) * SPAN
            dcum_scr[lo:hi] = mmf(upper, dcum_scr[lo:hi])
        da = dcum_scr[...]
        rate = hp[1:2]
        first = iota((rows, LANES), 1) < heads
        ddtp = jnp.where(first, (rate * da + ddt_scr[...]) * jax.nn.sigmoid(raw), 0.0)
        g_hp[...] = jnp.zeros_like(g_hp)
        g_hp[0:1] = jnp.sum(ddtp, axis=0, keepdims=True)
        g_hp[1:2] = jnp.sum(jnp.where(first, da * dt * rate, 0.0), axis=0, keepdims=True)
        dsh = low(
            jnp.concatenate(
                [dbc_scr[...], jnp.concatenate([ddtp, jnp.zeros((LANES, LANES), f32)], axis=0)],
                axis=1,
            )
        )
        g_b[...] = jnp.zeros_like(g_b)
        g_b[:, : dsh.shape[1]] = low(mm(nrmt[...], dsh))
        dn[...] += mmt(dsh[: rows + HALO], wb[...])


def whole(shape):
    return pl.BlockSpec(shape, lambda g: (0,) * len(shape))


def by_column(rows, width):
    return pl.BlockSpec((rows, width), lambda g: (0, g))


def kind_block(depth, pair):
    weights, kind = pair
    shape = weights.shape
    return pl.BlockSpec((None, shape[1], depth, shape[3]), lambda g: (g, 0, kind, 0))


def params(flops, moved):
    return dict(
        compiler_params=pltpu.CompilerParams(vmem_limit_bytes=VMEM),
        cost_estimate=pl.CostEstimate(flops=flops, bytes_accessed=moved, transcendentals=0),
    )


def struct(*shape, dtype=f32):
    return jax.ShapeDtypeStruct(shape, dtype)


def shift(x, axis, step):
    size = lax.axis_size(axis)
    return lax.ppermute(
        x, axis, [(i, i + step) for i in range(size) if 0 <= i + step < size]
    )


def bits_of(axis):
    return [(axis, b) for b in range(lax.axis_size(axis).bit_length() - 1)]


def exchange(x, axis, bit):
    return lax.ppermute(x, axis, [(i, i ^ (1 << bit)) for i in range(lax.axis_size(axis))])


def all_sum(x, order):
    for axis, bit in order:
        x = x + exchange(x, axis, bit)
    return x


def scatter_start(x, axes):
    names = [pair for axis in axes for pair in reversed(bits_of(axis))]
    return x.reshape((2,) * len(names) + x.shape[len(axes) :]), names


def outgoing(x, names, pair):
    axis, bit = pair
    mine = (lax.axis_index(axis) >> bit) & 1
    return lax.dynamic_index_in_dim(x, 1 - mine, names.index(pair), False)


def scatter_step(x, names, pair, got=None, kind=bf16):
    axis, bit = pair
    mine = (lax.axis_index(axis) >> bit) & 1
    if got is None:
        got = exchange(outgoing(x, names, pair), axis, bit)
    x = lax.dynamic_index_in_dim(x, mine, names.index(pair), False)
    x = (x.astype(f32) + got.astype(f32)).astype(kind)
    return x, [name for name in names if name != pair]


def scatter_rest(x, names, order, kind=bf16):
    for n, pair in enumerate(order):
        x, names = scatter_step(x, names, pair, None, f32 if n + 1 == len(order) else kind)
    return x


def carry_states(packed, axis, backward, beside=lambda got: (got, None)):
    size, at = lax.axis_size(axis), lax.axis_index(axis)
    count = packed.shape[0] - HALO

    def unpack(x):
        x = x.astype(f32)
        return x[:count], x[count : count + 1] + x[count + 1 : count + 2]

    total, factor = unpack(packed)
    prefix = jnp.zeros_like(total)
    prefix_factor = jnp.ones_like(factor)
    step = 1
    while step < size:
        upper = ((at // step) % 2) == 1
        follows = jnp.logical_not(upper) if backward else upper
        pairs = [(i, i ^ step) for i in range(size)]
        final = 2 * step >= size
        if final:
            pairs = [p for p in pairs if (p[0] > p[1]) == backward]
        got = lax.ppermute(packed, axis, pairs)
        if final:
            got, beside = beside(got)
        other, other_factor = unpack(got)
        prefix = jnp.where(follows, prefix_factor * other + prefix, prefix)
        if not final:
            prefix_factor = jnp.where(follows, prefix_factor * other_factor, prefix_factor)
            total = jnp.where(follows, factor * other + total, other_factor * total + other)
            factor = factor * other_factor
            high, rest = two(factor)
            packed = jnp.concatenate(
                [low(total), high, rest, jnp.zeros((HALO - 2, factor.shape[1]), bf16)], axis=0
            )
        step *= 2
    return low(prefix), beside


def body(
    hidden,
    segment_ids,
    in_gain,
    w_zx,
    w_bcdt,
    w_out,
    conv_x,
    conv_x_bias,
    conv_bc,
    conv_bc_bias,
    dt_bias,
    a_log,
    d_skip,
    out_gain,
    cotangent,
):
    layers, taps_n = conv_x.shape[0], conv_x.shape[1]
    groups, shards = lax.axis_size("tensor"), lax.axis_size("dp")
    tb, db = bits_of("tensor"), bits_of("dp")
    axes = ("tensor", "dp")
    order_x = tb + db
    order_y = tb[:1] + db[:1] + tb[1:] + db[1:]
    at_t = lax.axis_index("tensor")
    at_d = lax.axis_index("dp")
    own = dt_bias.shape[1]
    heads = own * groups
    width = out_gain.shape[1]
    full = width * groups
    rows, model = hidden.shape
    bc = conv_bc.shape[2]
    state_n = bc // 2
    depth = w_zx.shape[1]
    ext = rows + HALO
    chunks = rows // SPAN
    wide = bc + LANES
    copies = LANES // heads

    padded = jnp.pad(segment_ids.reshape(-1), (HALO, 0), constant_values=-1)
    seg = lax.dynamic_slice_in_dim(padded, at_t * rows, ext).astype(f32)
    segc = seg[:, None]
    segr = jnp.broadcast_to(seg[None, HALO:], (8, rows))

    heads_row = jnp.pad(
        jnp.concatenate([dt_bias, a_log, d_skip], axis=1), ((0, 0), (0, width - 3 * own))
    )
    pack = jnp.concatenate(
        [
            conv_x,
            conv_x_bias[:, None],
            out_gain[:, None],
            heads_row[:, None],
            jnp.zeros((layers, 1, width), f32),
        ],
        axis=1,
    )
    prm = lax.all_gather(pack, "tensor", axis=0, tiled=False)
    by_head = prm[:, :, 6]
    dtb = jnp.moveaxis(by_head[:, :, :own], 0, 1).reshape(layers, heads)
    alog = jnp.moveaxis(by_head[:, :, own : 2 * own], 0, 1).reshape(layers, heads)
    skip_ch = jnp.repeat(by_head[:, :, 2 * own : 3 * own], width // own, axis=2)
    prm = jnp.concatenate([prm[:, :, :6], skip_ch[:, :, None], prm[:, :, 7:]], axis=2)
    rate = -jnp.exp(alog)
    hp = jnp.concatenate(
        [
            jnp.tile(dtb, (1, copies))[:, None],
            jnp.tile(rate, (1, copies))[:, None],
            jnp.zeros((layers, 6, LANES), f32),
        ],
        axis=1,
    )
    cbc = jnp.concatenate(
        [conv_bc, conv_bc_bias[:, None], jnp.zeros((layers, 3, bc), f32)], axis=1
    )

    rows_b = depth // groups

    def shared_rows(i):
        both = jnp.concatenate([w_bcdt[i], in_gain[i][:, None]], axis=1)
        own_rows = lax.dynamic_slice_in_dim(both, at_t * rows_b, rows_b, 0)
        return jnp.pad(own_rows, ((0, 0), (0, width - both.shape[1])))

    def gather(pieces, after=None):
        local = jnp.concatenate(pieces, axis=0)
        if after is not None:
            local, _ = lax.optimization_barrier((local, after))
        got = lax.all_gather(local, ("tensor", "dp"), axis=0, tiled=False)
        return got.reshape((groups, shards) + local.shape)

    def spread_out(x, order):
        target = [pair for axis in axes for pair in reversed(bits_of(axis))]
        names = []
        for axis, bit in order:
            got = exchange(x, axis, bit)
            mine = (lax.axis_index(axis) >> bit) & 1
            dim = sum(target.index(name) < target.index((axis, bit)) for name in names)
            x = jnp.stack([jnp.where(mine == 0, x, got), jnp.where(mine == 0, got, x)], axis=dim)
            names.insert(dim, (axis, bit))
        return x.reshape((groups, shards) + x.shape[len(names) :])

    first = jnp.concatenate([w_zx[0, :, 1], shared_rows(0)], axis=0)
    half = width // 2
    ring = db[1:] + db[:1]
    right = spread_out(first[:, half:], ring[:-1] + tb[1:] + ring[-1:] + tb[:1])
    first = [spread_out(first[:, :half], ring + tb[1:] + tb[:1]), right]
    head = gather(
        [w_zx[0, :, 0], w_out[0]]
        + [w_zx[i, :, 1] for i in range(1, layers)]
        + [shared_rows(i) for i in range(1, layers)],
    )
    w_x = [[(part, 0) for part in first]] + [[(head, 1 + i)] for i in range(1, layers)]
    w_z, w_o = [(head, 0)], [(head, 1)]
    for i in range(1, layers):
        later = gather([w_zx[i, :, 0], w_out[i]])
        w_z.append((later, 0))
        w_o.append((later, 1))
    wbs, gains = [], []
    for i in range(layers):
        at = (1 + layers) * depth + (i - 1) * rows_b
        held = [part[:, :, depth:] for part in first] if i == 0 else [head[:, :, at : at + rows_b]]
        got = jnp.concatenate(
            [jnp.moveaxis(part, 0, 1).reshape(model, -1)[:, : 2 * half] for part in held], axis=1
        )
        wbs.append(
            jnp.concatenate(
                [got[:, :bc], jnp.tile(got[:, bc : bc + heads], (1, copies))], axis=1
            )
        )
        gains.append(got[:, bc + heads].astype(f32))

    small = [
        ((ext, wide), f32),
        ((rows, state_n), f32),
        ((rows, state_n), f32),
        ((state_n, rows), f32),
        ((state_n, rows), f32),
        ((rows, LANES), f32),
        ((LANES, rows), f32),
        ((rows, LANES), bf16),
        ((rows, LANES), bf16),
        ((rows, LANES), bf16),
        ((rows, LANES), bf16),
        ((rows, LANES), bf16),
    ]
    prm_spec = pl.BlockSpec((1, 8, width), lambda g: (g, 0, 0))
    saved = []
    stream = hidden
    for i in range(layers):
        rinv = lax.rsqrt(jnp.mean(stream * stream, axis=-1, keepdims=True) + epsilon)
        normed = (stream * rinv * gains[i]).astype(bf16)
        before = shift(normed[rows - HALO :], "tensor", 1)
        nrmt = jnp.concatenate(
            [normed, before, jnp.zeros((LANES - HALO, model), bf16)], axis=0
        ).T
        wb, pr = wbs[i], prm[:, i]
        flops = 2 * ext * model * (full + wide)
        outs = pl.pallas_call(
            partial(scan_in_kernel, heads, own, taps_n, len(w_x[i])),
            grid=(groups,),
            in_specs=[
                whole((HALO, model)),
                whole((rows, model)),
                *[kind_block(depth, part) for part in w_x[i]],
                whole((model, wide)),
                prm_spec,
                whole((8, bc)),
                whole((8, LANES)),
                whole((ext, 1)),
                whole((8, rows)),
            ],
            out_specs=[
                by_column(rows, width),
                by_column(ext, width),
                by_column(state_n + HALO, width),
                by_column(8, width),
            ]
            + [whole(s) for s, _ in small],
            out_shape=[
                struct(rows, full),
                struct(ext, full),
                struct(state_n + HALO, full, dtype=bf16),
                struct(8, full),
            ]
            + [struct(*s, dtype=d) for s, d in small],
            scratch_shapes=[
                pltpu.VMEM((chunks, SPAN, SPAN), f32),
                pltpu.VMEM((chunks, SPAN, SPAN), f32),
            ],
            name="scan_in",
            **params(3 * flops, 4 * rows * full * 3),
        )(before, normed, *[part for part, _ in w_x[i]], wb, pr, cbc[i], hp[i], segc, segr)
        y_loc, xin, state, ftot = outs[:4]
        rest = outs[4:]
        shared, b_m, c_m, b_t, c_t, dtp, cumt, dts, es, fs, fd, cums = rest
        s_in, _ = carry_states(state, "tensor", False)
        z, y, branch, grms, nxt = pl.pallas_call(
            partial(gate_kernel, heads, own, full),
            grid=(groups,),
            in_specs=[
                whole((rows, model)),
                kind_block(depth, w_z[i]),
                pl.BlockSpec((groups, shards, depth, width), lambda g, k=w_o[i][1]: (0, 0, k, 0)),
                by_column(rows, width),
                whole((rows, state_n)),
                whole((rows, LANES)),
                by_column(state_n, width),
                whole((groups, 8, width)),
                whole((rows, model)),
            ],
            out_specs=[
                by_column(rows, width),
                by_column(rows, width),
                whole((rows, model)),
                whole((rows, LANES)),
                whole((rows, model)),
            ],
            out_shape=[
                struct(rows, full),
                struct(rows, full),
                struct(rows, model),
                struct(rows, LANES),
                struct(rows, model),
            ],
            scratch_shapes=[
                pltpu.VMEM((rows, LANES), f32),
                pltpu.VMEM((groups, rows, width), f32),
            ],
            name="gate",
            **params(4 * rows * model * full, 4 * rows * full * 5),
        )(normed, w_z[i][0], w_o[i][0], y_loc, c_m, fd, s_in, pr, stream)
        saved.append((stream, rinv, nrmt, xin, ftot, rest, s_in, z, y, branch, grms))
        stream = nxt

    def grad_block(count):
        return pl.BlockSpec((None, shards, count, width), lambda g: (g, 0, 0, 0))

    def finish(i, grad, dn, after):
        stream_in, rinv = saved[i][:2]
        dnormed = jnp.concatenate(
            [dn[: rows - HALO], dn[rows - HALO : rows] + after], axis=0
        )
        scaled_in = stream_in * rinv
        gain_grads.append(jnp.sum(dnormed * scaled_in, axis=0))
        scaled = dnormed * gains[i]
        return grad + rinv * (
            scaled - scaled_in * jnp.mean(scaled * scaled_in, axis=-1, keepdims=True)
        )

    def keep_small(g_gain, g_prm, g_cbc, g_hp):
        prm_grads.append(g_prm.at[:, 5].set(g_gain[0].reshape(groups, width)))
        cbc_grads.append(g_cbc)
        hp_grads.append(g_hp)

    def stacked(items):
        return jnp.stack(items[::-1], axis=0)

    grad = cotangent
    x_part = None
    gain_grads, prm_grads, cbc_grads, hp_grads = [], [], [], []

    for i in reversed(range(layers)):
        stream_in, rinv, nrmt, xin, ftot, rest, s_in, z, y, branch, grms = saved[i]
        shared, b_m, c_m, b_t, c_t, dtp, cumt, dts, es, fs, fd, cums = rest
        wb, pr = wbs[i], prm[:, i]
        dbr = grad.astype(bf16)
        if x_part is not None:
            dbr, x_part, x_send = lax.optimization_barrier((dbr, x_part, x_send))
            x_got = exchange(x_send, *tb[1])
        g_zo, dy, dnz, dstate, g_gain = pl.pallas_call(
            partial(gate_back_kernel, heads, own, full),
            grid=(groups,),
            in_specs=[
                whole((rows, model)),
                whole((model, rows)),
                whole((rows, model)),
                kind_block(depth, w_o[i]),
                kind_block(depth, w_z[i]),
                by_column(rows, width),
                by_column(rows, width),
                whole((rows, LANES)),
                whole((model, rows + LANES)),
                whole((state_n, rows)),
                whole((rows, LANES)),
                prm_spec,
            ],
            out_specs=[
                grad_block(2 * depth),
                by_column(rows, width),
                whole((rows, model)),
                by_column(state_n + HALO, width),
                by_column(8, width),
            ],
            out_shape=[
                struct(groups, shards, 2 * depth, width, dtype=bf16),
                struct(rows, full),
                struct(rows, model),
                struct(state_n + HALO, full, dtype=bf16),
                struct(8, full),
            ],
            scratch_shapes=[pltpu.VMEM((rows, LANES), f32)],
            name="gate_back",
            **params(8 * rows * model * full, 4 * rows * full * 6),
        )(dbr, dbr.T, branch, w_o[i][0], w_z[i][0], z, y, grms, nrmt, c_t, fd, pr)
        if x_part is not None:
            g_zo, dy, dnz, dstate, g_gain, x_got = lax.optimization_barrier(
                (g_zo, dy, dnz, dstate, g_gain, x_got)
            )
        chains = []
        for part, order in (
            (g_zo[:, :, :depth], order_x),
            (g_zo[:, :, depth:], order_y if i == 0 else order_x),
        ):
            part, names = scatter_step(*scatter_start(part, axes), order[0])
            chains.append((part, names, order[1], outgoing(part, names, order[1])))
        (z_new, z_names, z_pair, z_send), (o_new, o_names, o_pair, o_send) = chains
        held = [z_new, o_new, z_send, o_send]
        if x_part is not None:
            x_part, _ = scatter_step(x_part, x_names, tb[1], x_got)
            held.append(jnp.concatenate([z_part, o_part, x_part], axis=len(db)))
        ds_in, held = carry_states(
            dstate, "tensor", True, lambda got: lax.optimization_barrier((got, held))
        )
        z_part, o_part, z_send, o_send = held[:4]
        if x_part is not None:
            later_sum = lax.psum_scatter(
                held[4].reshape((shards,) + held[4].shape[len(db) :]),
                "dp",
                scatter_dimension=0,
                tiled=False,
            )
        z_got = exchange(z_send, *z_pair)
        o_got = exchange(o_send, *o_pair)
        g_x, g_b, dn, g_prm, g_cbc, g_hp = pl.pallas_call(
            partial(scan_back_kernel, heads, own, taps_n, len(w_x[i])),
            grid=(groups,),
            in_specs=[
                by_column(ext, width),
                by_column(rows, width),
                by_column(rows, width),
                by_column(state_n, width),
                by_column(state_n, width),
                whole((rows, model)),
                *[kind_block(depth, part) for part in w_x[i]],
                whole((model, wide)),
                prm_spec,
                whole((8, bc)),
                whole((8, LANES)),
                whole((ext, 1)),
                whole((8, rows)),
                whole((model, rows + LANES)),
            ]
            + [whole(s) for n, (s, _) in enumerate(small) if n != 10],
            out_specs=[
                grad_block(depth),
                whole((model, width)),
                whole((ext, model)),
                pl.BlockSpec((1, 8, width), lambda g: (g, 0, 0)),
                whole((8, bc)),
                whole((8, LANES)),
            ],
            out_shape=[
                struct(groups, shards, depth + rows_b, width, dtype=bf16),
                struct(model, width, dtype=bf16),
                struct(ext, model),
                struct(groups, 8, width),
                struct(8, bc),
                struct(8, LANES),
            ],
            scratch_shapes=[
                pltpu.VMEM((chunks, SPAN, SPAN), f32),
                pltpu.VMEM((chunks, SPAN, SPAN), f32),
                pltpu.VMEM((chunks, SPAN, SPAN), f32),
                pltpu.VMEM((rows, state_n), f32),
                pltpu.VMEM((rows, state_n), f32),
                pltpu.VMEM((rows, LANES), f32),
                pltpu.VMEM((rows, LANES), f32),
                pltpu.VMEM((rows + LANES, width), f32),
                pltpu.VMEM((rows + LANES, bc), f32),
                pltpu.VMEM((rows, width), f32),
            ],
            name="scan_back",
            **params(8 * rows * model * full, 4 * rows * full * 6),
        )(
            xin, dy, y, s_in, ds_in, dnz, *[part for part, _ in w_x[i]], wb, pr, cbc[i], hp[i], segc, segr, nrmt,
            shared, b_m, c_m, b_t, c_t, dtp, cumt, dts, es, fs, cums,
        )
        g_x, g_b, dn, g_prm, g_cbc, g_hp, z_got, o_got = lax.optimization_barrier(
            (g_x, g_b, dn, g_prm, g_cbc, g_hp, z_got, o_got)
        )
        z_part, z_names = scatter_step(z_part, z_names, z_pair, z_got)
        o_part, o_names = scatter_step(o_part, o_names, o_pair, o_got)
        parts_b = jnp.moveaxis(g_b.reshape(shards, groups, rows_b, width), 1, 0)
        g_x = lax.dynamic_update_slice(g_x, parts_b, (0, 0, depth, 0))
        if i > 0:
            x_part, x_names = scatter_step(*scatter_start(g_x, axes), tb[0])
            x_send = outgoing(x_part, x_names, tb[1])
        else:
            break
        after = shift(dn[rows:], "tensor", -1)
        grad = finish(i, grad, dn, after)
        keep_small(g_gain, g_prm, g_cbc, g_hp)

    def together(sends, pairs, beside=()):
        sends = lax.optimization_barrier(sends)
        gots = []
        for send, pair in zip(sends, pairs):
            if pair is None:
                gots.append(shift(send, "tensor", -1))
            elif len(pair) == 3:
                size = lax.axis_size(pair[0])
                gots.append(lax.ppermute(send, pair[0], [(k, k ^ pair[1]) for k in range(size)]))
            else:
                gots.append(exchange(send, *pair))
        return lax.optimization_barrier([*gots, *beside])

    keep_small(g_gain, g_prm, g_cbc, g_hp)
    x_full, x_names = scatter_start(g_x, axes)
    x_got, after = together([outgoing(x_full, x_names, tb[0]), dn[rows:]], [tb[0], None])
    x_part, x_names = scatter_step(x_full, x_names, tb[0], x_got)
    chains = [
        [x_part[..., :half], x_names, list(order_x[1:])],
        [x_part[..., half:], x_names, list(order_y[1:])],
    ]
    chains.append([z_part, z_names, list(order_x[2:])])
    chains.append([o_part, o_names, [p for p in order_y if p in o_names]])
    grad = finish(0, grad, dn, after)
    rest_sum = jnp.concatenate(
        [
            stacked(gain_grads).reshape(-1),
            stacked(cbc_grads).reshape(-1),
            stacked(hp_grads).reshape(-1),
        ]
    ).reshape(-1, width)
    small, small_names = scatter_start(stacked(prm_grads).swapaxes(0, 1), ("tensor",))
    rounds = [[bit] for bit in tb + db[:-2]] + [db[-2:]]
    while rounds or any(order for _, _, order in chains):
        live = [chain for chain in chains if chain[2]]
        bits = rounds.pop(0) if rounds else []
        sends = [outgoing(part, names, order[0]) for part, names, order in live]
        pairs = [order[0] for _, _, order in live]
        beside = []
        if bits and bits[0] in tb:
            if bits[0] == tb[0]:
                beside = [later_sum]
            leaving = outgoing(small, small_names, bits[0])
            sends.append(jnp.concatenate([leaving.reshape(-1, width), rest_sum], axis=0))
            pairs.append(bits[0])
        elif bits:
            if small is not None:
                rest_sum = jnp.concatenate([small.reshape(-1, width), rest_sum], axis=0)
                small = None
            steps = [0]
            for _, bit in bits:
                steps += [step | (1 << bit) for step in steps]
            for step in steps[1:]:
                sends.append(rest_sum)
                pairs.append((bits[0][0], step, None))
        gots = together(sends, pairs, beside)
        if beside:
            *gots, later_sum = gots
        for chain, got in zip(live, gots):
            part, names, order = chain
            kind = f32 if len(order) == 1 else bf16
            chain[0], chain[1] = scatter_step(part, names, order[0], got, kind)
            chain[2] = order[1:]
        gots = gots[len(live) :]
        if bits and bits[0] in tb:
            count = gots[0].shape[0] - rest_sum.shape[0]
            kept_shape = outgoing(small, small_names, bits[0]).shape
            arrived = gots[0][:count].reshape(kept_shape)
            small, small_names = scatter_step(small, small_names, bits[0], arrived, f32)
            rest_sum = rest_sum + gots[0][count:]
        else:
            for got in gots:
                rest_sum = rest_sum + got
    x_done = jnp.concatenate([chains[0][0], chains[1][0]], axis=1)
    z_done, o_done = chains[2][0], chains[3][0]
    done = [jnp.concatenate([z_done, o_done, x_done], axis=0), later_sum.astype(f32)]
    mine = rest_sum[: 8 * layers].reshape(layers, 8, width)
    flat = rest_sum[8 * layers :].reshape(-1)
    gain_all = flat[: layers * model].reshape(layers, model)
    flat = flat[layers * model :]
    cbc_all = flat[: layers * 8 * bc].reshape(layers, 8, bc)
    hp_all = flat[layers * 8 * bc :].reshape(layers, 8, LANES)
    per = model // (groups * shards)
    grad_in_gain = lax.dynamic_slice_in_dim(gain_all, (at_d * groups + at_t) * per, per, 1)
    heads_mine = lax.dynamic_slice_in_dim(hp_all, at_t * own, own, 2)
    grad_w_zx = jnp.stack(
        [jnp.stack([d[:depth], d[2 * depth : 3 * depth]], axis=1) for d in done], axis=0
    )
    grad_w_out = jnp.stack([d[depth : 2 * depth] for d in done], axis=0)
    grad_w_bcdt = jnp.stack([d[3 * depth :, : bc + heads] for d in done], axis=0)
    return (
        stream,
        grad,
        grad_in_gain,
        grad_w_zx,
        grad_w_bcdt,
        grad_w_out,
        mine[:, :taps_n],
        mine[:, taps_n],
        cbc_all[:, :taps_n],
        cbc_all[:, taps_n],
        heads_mine[:, 0],
        heads_mine[:, 1],
        mine[:, 6].reshape(layers, own, width // own).sum(axis=-1),
        mine[:, 5],
    )


def solution(mesh):
    placed = (
        P(("dp", "tensor"), None),
        P("dp", None),
        P(None, "dp"),
        P(None, "dp", None, "tensor"),
        P(None, "dp", None),
        P(None, "dp", "tensor"),
        P(None, None, "tensor"),
        P(None, "tensor"),
        P(),
        P(),
        P(None, "tensor"),
        P(None, "tensor"),
        P(None, "tensor"),
        P(None, "tensor"),
        P(("dp", "tensor"), None),
    )
    return jax.shard_map(
        body,
        mesh=mesh,
        in_specs=placed,
        out_specs=(
            P(("dp", "tensor"), None),
            P(("dp", "tensor"), None),
            P(None, ("dp", "tensor")),
            P(None, "dp", None, "tensor"),
            P(None, ("dp", "tensor"), None),
            P(None, "dp", "tensor"),
            P(None, None, "tensor"),
            P(None, "tensor"),
            P(),
            P(),
            P(None, "tensor"),
            P(None, "tensor"),
            P(None, "tensor"),
            P(None, "tensor"),
        ),
        check_vma=False,
    )
```
